128 devices in a mesh: lat: 16 (over y, x), lon: 8 (over z, core).
Axes of the slice: x: 4, y: 4, z: 4, core: 2. Of those that a mesh axis runs over, the one named last changes fastest.
Arguments:
- state_start: float32 [6, 2048, 7200], P(None, 'lat', 'lon'), may hold values from -6 to 6
- state_section: float32 [6, 2048, 7200], P(None, 'lat', 'lon'), may hold values from -6 to 6
- zonal_courant: float32 [6, 2048, 7200], P(None, 'lat', 'lon'), may hold values from -0.4 to 0.4
- merid_courant: float32 [6, 2048, 7200], P(None, 'lat', 'lon'), may hold values from -0.4 to 0.4
- cutoffs: int32 [2048], replicated, may hold values from 64 to 511, as said below
- nest_values: float32 [2, 6, 128, 256], P(None, None, ('lat', 'lon')), may hold values from -6 to 6
- nest_corners: int32 [2, 2], replicated, may hold values from 0 to 6944, as said below
Outputs:
- new_state: float32 [6, 2048, 7200], P(None, 'lat', 'lon')
The draws below stay inside these ranges and needn't reach their ends.
Inputs may be any that keep to these rules, and one draw needn't show every extreme that they name: `cutoffs`: only rows poleward of 45 degrees are read; among them the value 512 - 1 occurs in a southern row and 64 in a northern row. `nest_corners`: block 0 lies wholly in the southern half of the rows, block 1 wholly in the northern half; each block lies inside the grid without crossing the longitude seam; one entry always equals the stated most.
All inputs are finite; a program needn't handle non-finite values.
Results may differ from the reference program's by a relative error of at most 0.000067.
Values sent between devices are 32-bit elements; how exact they have to be, the bound alone decides.
A program may use at most 128 MiB of HBM per device.

```python
import math
import jax
import jax.numpy as jnp
from jax import lax

LEV = 6
NLON = 7200
KMAX = 512
NEST = 2
NB_LON = 256
NLAT = 2048
NB_LAT = 128


def draw_cutoffs(key, part):
    values = jax.random.randint(key, (NLAT,), KMAX // 8, KMAX, dtype=jnp.int32)
    south_pick = jax.random.randint(jax.random.fold_in(key, 7), (), 0, NLAT // 4, dtype=jnp.int32)
    north_pick = jax.random.randint(jax.random.fold_in(key, 11), (), 3 * NLAT // 4, NLAT, dtype=jnp.int32)
    values = values.at[south_pick].set(KMAX - 1)
    return values.at[north_pick].set(KMAX // 8)


def draw_nest_corners(key, part):
    subkeys = jax.random.split(key, 4)
    south_row = jax.random.randint(subkeys[0], (), 0, NLAT // 2 - NB_LAT + 1, dtype=jnp.int32)
    north_row = jax.random.randint(subkeys[1], (), NLAT // 2, NLAT - NB_LAT + 1, dtype=jnp.int32)
    west_cols = jax.random.randint(subkeys[2], (2,), 0, NLON - NB_LON + 1, dtype=jnp.int32)
    east_pick = jax.random.randint(subkeys[3], (), 0, 2, dtype=jnp.int32)
    if NLAT - NB_LAT >= NLON - NB_LON:
        north_row = jnp.int32(NLAT - NB_LAT) + 0 * north_row
    else:
        west_cols = jnp.where(jnp.arange(2, dtype=jnp.int32) == east_pick, jnp.int32(NLON - NB_LON), west_cols)
    return jnp.stack([jnp.stack([south_row, west_cols[0]]), jnp.stack([north_row, west_cols[1]])]).astype(jnp.int32)


def levels(rng, shape, pieces, smallest, top_value):
    def one(position, shards_of):
        draws = jax.random.uniform(jax.random.fold_in(jax.random.fold_in(rng, 6), position), (shards_of,), jnp.float32, smallest / len(pieces), top_value / len(pieces))
        return jnp.repeat(jnp.exp(draws), shape[position] // shards_of).reshape((-1,) + (1,) * (len(shape) - position - 1))

    loudness = one(*pieces[0])
    for cut in pieces[1:]:
        loudness = loudness * one(*cut)
    return loudness


def gaussian(rng, extent, scale, reach, pieces=(), kind=jnp.bfloat16):
    gain = levels(rng, extent, pieces, -0.22, 0.18) if pieces else 1.0
    result = jax.random.normal(rng, extent, jnp.float32) * scale * gain
    return jnp.minimum(jnp.maximum(result, -reach), reach).astype(kind)


def setup_inputs(seed: int = 0) -> dict:
    seeds = jax.random.split(jax.random.key(seed), 8)
    return {
        "state_start": gaussian(seeds[0], (LEV, NLAT, NLON), 1.0, 6.0, ((1, 16), (2, 8)), jnp.float32),
        "state_section": gaussian(seeds[1], (LEV, NLAT, NLON), 1.0, 6.0, ((1, 16), (2, 8)), jnp.float32),
        "zonal_courant": jnp.clip(jax.random.uniform(seeds[2], (LEV, NLAT, NLON), jnp.float32, -0.4, 0.4) * levels(seeds[2], (LEV, NLAT, NLON), ((1, 16), (2, 8)), -0.4, 0.0), -0.4, 0.4),
        "merid_courant": jnp.clip(jax.random.uniform(seeds[3], (LEV, NLAT, NLON), jnp.float32, -0.4, 0.4) * levels(seeds[3], (LEV, NLAT, NLON), ((1, 16), (2, 8)), -0.4, 0.0), -0.4, 0.4),
        "cutoffs": draw_cutoffs(jax.random.fold_in(seeds[7], 71), 0),
        "nest_values": gaussian(seeds[5], (NEST, LEV, NB_LAT, NB_LON), 1.0, 6.0, ((2, 128),), jnp.float32),
        "nest_corners": draw_nest_corners(jax.random.fold_in(seeds[7], 71), 0),
    }


precise = lax.Precision.HIGHEST


def edge_values(indices, total):
    angles = indices.astype(jnp.float32) * (math.pi / total) - math.pi / 2
    return jnp.where((indices == 0) | (indices == total), jnp.float32(0.0), jnp.cos(angles))


def center_values(indices, total):
    angles = (indices.astype(jnp.float32) + 0.5) * (math.pi / total) - math.pi / 2
    return jnp.cos(angles)


def dft_tables(length, wave_count):
    places = jnp.arange(length, dtype=jnp.int32)
    numbers = jnp.arange(wave_count, dtype=jnp.int32)
    phases = (places[:, None] * numbers[None, :]) % length
    angles = phases.astype(jnp.float32) * (2 * math.pi / length)
    return jnp.cos(angles), jnp.sin(angles)


def lowpass(signal, cutoff, cosine_table, sine_table):
    length = signal.shape[-1]
    wave_count = cosine_table.shape[1]
    numbers = jnp.arange(wave_count, dtype=jnp.int32)
    base_weight = jnp.where(numbers == 0, jnp.float32(1.0), jnp.float32(2.0)) / length
    weights = jnp.where(numbers[None, :] <= cutoff[:, None], base_weight[None, :], jnp.float32(0.0))
    cos_part = jnp.dot(signal, cosine_table, precision=precise, preferred_element_type=jnp.float32) * weights
    sin_part = jnp.dot(signal, sine_table, precision=precise, preferred_element_type=jnp.float32) * weights
    return jnp.dot(cos_part, cosine_table.T, precision=precise, preferred_element_type=jnp.float32) + jnp.dot(sin_part, sine_table.T, precision=precise, preferred_element_type=jnp.float32)


def reference(state_start, state_section, zonal_courant, merid_courant, cutoffs, nest_values, nest_corners):
    lat_total = state_section.shape[1]
    lon_total = state_section.shape[2]
    edges = edge_values(jnp.arange(lat_total + 1, dtype=jnp.int32), lat_total)
    centers = center_values(jnp.arange(lat_total, dtype=jnp.int32), lat_total)
    tracer = state_section
    zonal_flux = 0.25 * (zonal_courant + jnp.roll(zonal_courant, -1, 2)) * (tracer + jnp.roll(tracer, -1, 2))
    zonal_div = zonal_flux - jnp.roll(zonal_flux, 1, 2)
    padding = ((0, 0), (1, 1), (0, 0))
    tracer_pad = jnp.pad(tracer, padding)
    merid_pad = jnp.pad(merid_courant, padding)
    merid_flux = 0.25 * (merid_pad[:, :-1] + merid_pad[:, 1:]) * (tracer_pad[:, :-1] + tracer_pad[:, 1:]) * edges[None, :, None]
    merid_div = (merid_flux[:, 1:] - merid_flux[:, :-1]) / centers[None, :, None]
    sectioned = 0.75 * state_start + 0.25 * (tracer - zonal_div - merid_div)
    quarter = lat_total // 4
    cosine_table, sine_table = dft_tables(lon_total, KMAX)
    polar_cut = jnp.concatenate([cutoffs[:quarter], cutoffs[lat_total - quarter:]])

    def filter_level(field):
        polar_rows = jnp.concatenate([field[:quarter], field[lat_total - quarter:]], axis=0)
        smooth = lowpass(polar_rows, polar_cut, cosine_table, sine_table)
        return jnp.concatenate([smooth[:quarter], field[quarter:lat_total - quarter], smooth[quarter:]], axis=0)

    filtered = lax.map(filter_level, sectioned)
    for nest_index in range(NEST):
        corner_row = nest_corners[nest_index, 0].astype(jnp.int32)
        corner_col = nest_corners[nest_index, 1].astype(jnp.int32)
        filtered = lax.dynamic_update_slice(filtered, nest_values[nest_index].astype(filtered.dtype), (jnp.int32(0), corner_row, corner_col))
    return filtered
```

```python
import math

import jax
import jax.numpy as jnp
import ml_dtypes
import numpy as np
from jax import lax
from jax.experimental import pallas as pl
from jax.experimental.pallas import tpu as pltpu
from jax.sharding import PartitionSpec as P

LEV, NLAT, NLON, KMAX = 6, 2048, 7200, 512
BANDS, SEGS = 16, 8
ROWS, SEG = NLAT // BANDS, NLON // SEGS
RANK = 160
PART = RANK // 4
CHUNKS, PAIR = 3, 2
STEP, STEPS = 32, 29
TALL = STEP * STEPS + 8
WIDE = 1024
MESH = pl.DeviceIdType.MESH
BF = ml_dtypes.bfloat16


def tri_solve(diag, off, shift, rhs):
    n, r = rhs.shape
    b = rhs.copy()
    d, u1, u2 = (np.zeros((n, r)) for _ in range(3))
    cd, cu, cb = diag[0] - shift, np.full(r, off[0]), b[0]
    for j in range(n - 1):
        nd, nu, sub = diag[j + 1] - shift, off[j + 1] if j + 2 < n else 0.0, off[j]
        swap = np.abs(sub) > np.abs(cd)
        p = np.where(swap, sub, np.where(cd == 0, 1e-30, cd))
        pu1, pu2, pb = np.where(swap, nd, cu), np.where(swap, nu, 0.0), np.where(swap, b[j + 1], cb)
        o, ou1 = np.where(swap, cd, sub), np.where(swap, cu, nd)
        ou2, ob = np.where(swap, 0.0, nu), np.where(swap, cb, b[j + 1])
        f = o / p
        d[j], u1[j], u2[j], b[j] = p, pu1, pu2, pb
        cd, cu, cb = ou1 - f * pu1, ou2 - f * pu2, ob - f * pb
    d[n - 1] = np.where(np.abs(cd) < 1e-20, 1e-20, cd)
    b[n - 1] = cb
    x = np.zeros((n, r))
    x[n - 1] = b[n - 1] / d[n - 1]
    x[n - 2] = (b[n - 2] - u1[n - 2] * x[n - 1]) / d[n - 2]
    for j in range(n - 3, -1, -1):
        x[j] = (b[j] - u1[j] * x[j + 1] - u2[j] * x[j + 2]) / d[j]
    return x


def slepian(length, width, rank):
    i = np.arange(length, dtype=np.float64)
    diag = ((length - 1 - 2 * i) / 2) ** 2 * np.cos(2 * np.pi * width)
    off = (i * (length - i) / 2)[1:]
    off2 = np.concatenate([[0.0], off**2])
    bound = np.abs(diag).max() + 2 * off.max()
    low, high, want = np.full(rank, -bound), np.full(rank, bound), np.arange(rank)
    for _ in range(70):
        mid = 0.5 * (low + high)
        above, q = np.zeros(rank, dtype=np.int64), np.ones(rank)
        for j in range(length):
            q = diag[j] - mid - off2[j] / q
            q = np.where(q == 0.0, 1e-300, q)
            above += q > 0
        up = above > want
        low, high = np.where(up, mid, low), np.where(up, high, mid)
    x = np.ones((length, rank)) + 0.3 * np.cos(i * i)[:, None]
    for _ in range(4):
        x = tri_solve(diag, off, 0.5 * (low + high), x)
        x = x / np.sqrt((x * x).sum(0))
    return x


def split(x):
    hi = x.astype(BF)
    return hi, (x - hi.astype(np.float64)).astype(BF)


def make_tables():
    basis = slepian(SEG, 512.0 / NLON, RANK)
    k, i = np.arange(KMAX), np.arange(SEG)
    waves = np.exp(-2j * np.pi * ((i[:, None] * k[None, :]) % NLON) / NLON)
    v = np.einsum("ir,ik->rk", basis, waves)
    weight = np.where(k == 0, 1.0, 2.0) / NLON
    uh, ul = split(basis)
    ut = np.zeros((2 * RANK, WIDE), BF)
    ut[:RANK, :SEG], ut[RANK:, :SEG] = uh.T, ul.T
    eu = np.zeros((STEP * STEPS, 512), BF)
    eu[:SEG, :RANK], eu[:SEG, RANK : 2 * RANK], eu[:SEG, 2 * RANK : 3 * RANK] = uh, uh, ul
    pt = np.zeros((4, 256, WIDE), BF)
    qt = np.zeros((4, 2 * RANK, 768), BF)
    for g in range(4):
        s1, s2 = g, (4 if g == 0 else 8 - g)
        k1, k2 = np.arange(64) * 8 + s1, np.arange(64) * 8 + s2
        v1, v2 = v[:, k1], v[:, k2]
        w1, w2 = weight[k1], weight[k2]
        z = np.zeros((RANK, 64))
        if g == 0:
            p = np.block([[v1.real, z, v1.imag, z], [z, v2.real, z, v2.imag]])
            q = np.block([[v1.real * w1, z, v1.imag * w1, z], [z, v2.real * w2, z, v2.imag * w2]])
        else:
            p = np.block([[v1.real, v2.real, v1.imag, v2.imag], [-v1.imag, v2.imag, v1.real, -v2.real]])
            q = np.block(
                [
                    [v1.real * w1, v2.real * w2, v1.imag * w1, v2.imag * w2],
                    [-v1.imag * w1, v2.imag * w2, v1.real * w1, -v2.real * w2],
                ]
            )
        ph, pl_ = split(p.T)
        pt[g, :, :320], pt[g, :, 320:640], pt[g, :, 640:960] = ph, ph, pl_
        qh, ql = split(q)
        qt[g, :, :256], qt[g, :, 256:512], qt[g, :, 512:] = qh, qh, ql
    step = np.float32(math.pi / NLAT)
    half = np.float32(math.pi / 2)
    e = np.arange(NLAT + 1)
    edge = np.cos((e.astype(np.float32) * step - half).astype(np.float64)).astype(np.float32)
    edge[0] = edge[-1] = 0.0
    center = np.cos(((np.arange(NLAT).astype(np.float32) + np.float32(0.5)) * step - half).astype(np.float64))
    rc = np.zeros((BANDS, 8, ROWS), np.float32)
    for b in range(BANDS):
        r0 = b * ROWS
        rc[b, 0] = 0.0625 * edge[r0 + 1 : r0 + ROWS + 1]
        rc[b, 1] = (1.0 / center[r0 : r0 + ROWS]).astype(np.float32)
        rc[b, 2] = 0.0625 * edge[r0]
        rc[b, 3] = 0.0625 * edge[r0 + ROWS]
    return ut, eu, pt, qt, rc


def lanes(shape):
    return lax.broadcasted_iota(jnp.int32, shape, len(shape) - 1)


def hi_lo(x):
    hi = x.astype(jnp.bfloat16)
    return hi, (x - hi.astype(jnp.float32)).astype(jnp.bfloat16)


def dot(a, b):
    return jnp.dot(a, b, preferred_element_type=jnp.float32)


def section_kernel(
    start, sec, zon, mer, ut_h, pt_h, qt_h, cut, rc, nest,
    zout, sect, nestg,
    sb, tb, zb, mb, ut, pt, qt, sh, sl, pk, pkr, fl, lh,
    fsend, recv, bsend, nsend, ngat, nasm,
    ld, tabs, psend, precv, lsend, lrecv, fs, fr, bs, br, n1s, n1r, n2s, n2r, osem, zsem,
):
    lat, lon = lax.axis_index("lat"), lax.axis_index("lon")
    polar = (lat < BANDS // 4) | (lat >= BANDS - BANDS // 4)

    loads = []
    for c in range(CHUNKS):
        pair = pl.ds(PAIR * c, PAIR)
        loads.append([])
        for a, (src, dst) in enumerate(((sec, tb), (mer, mb), (zon, zb), (start, sb))):
            copy = pltpu.make_async_copy(src.at[pair], dst.at[pair, pl.ds(0, SEG)], ld.at[c, a])
            copy.start()
            loads[c].append(copy)
    tables = [
        pltpu.make_async_copy(src, dst, tabs.at[n]) for n, (src, dst) in enumerate(((ut_h, ut), (pt_h, pt), (qt_h, qt)))
    ]
    for copy in tables:
        copy.start()

    barrier = pltpu.get_barrier_semaphore()
    for k in range(1, SEGS):
        pl.semaphore_signal(barrier, inc=1, device_id=(lat, lax.rem(lon + k, SEGS)), device_id_type=MESH)
    for k in range(1, BANDS):
        pl.semaphore_signal(barrier, inc=1, device_id=(lax.rem(lat + k, BANDS), lon), device_id_type=MESH)
    for n in range(12):
        nsend[n : n + 1, :] = nest[n // 6, n % 6]
    nsend[12:16, :] = jnp.zeros((4, 256), jnp.float32)
    for buf in (tb, zb, mb, sb):
        for lev in range(LEV):
            buf[lev, SEG:TALL, :] = jnp.zeros((TALL - SEG, ROWS), jnp.float32)
    sh[STEP * STEPS :, :] = jnp.zeros((WIDE - STEP * STEPS, 256), jnp.bfloat16)
    sl[STEP * STEPS :, :] = jnp.zeros((WIDE - STEP * STEPS, 256), jnp.bfloat16)
    pl.semaphore_wait(barrier, SEGS - 1 + BANDS - 1)

    left, right = lax.rem(lon + SEGS - 1, SEGS), lax.rem(lon + 1, SEGS)
    lon_copies = []
    for a, src in enumerate((sec, zon)):
        for way, (row, to) in enumerate(((0, left), (SEG - 1, right))):
            copy = pltpu.make_async_remote_copy(
                src_ref=src.at[:, pl.ds(row, 1), :], dst_ref=lh.at[a, way], send_sem=lsend.at[a, way],
                recv_sem=lrecv.at[a, way], device_id=(lat, to), device_id_type=MESH,
            )
            copy.start()
            lon_copies.append(copy)
    nest_copies = []
    for k in range(1, SEGS):
        copy = pltpu.make_async_remote_copy(
            src_ref=nsend, dst_ref=ngat.at[lon], send_sem=n1s.at[k], recv_sem=n1r.at[k],
            device_id=(lat, lax.rem(lon + k, SEGS)), device_id_type=MESH,
        )
        copy.start()
        nest_copies.append(copy)
    ngat[lon] = nsend[...]

    before, after = lax.rem(lat + BANDS - 1, BANDS), lax.rem(lat + 1, BANDS)
    lane = lanes((STEP, ROWS))
    even = (lane & 1) == 0
    lat_copies = []
    for c in range(CHUNKS):
        loads[c][0].wait()
        loads[c][1].wait()

        def pack(b, acc, c=c):
            out = []
            for buf, x in zip((tb, mb), acc):
                for h in range(PAIR):
                    v = buf[PAIR * c + h, pl.ds(pl.multiple_of(b * STEP, STEP), STEP), :]
                    x = jnp.where((lane >> 1) == 2 * b + h, pltpu.roll(v, lax.rem(4 * b + 2 * h + 1, ROWS), 1), x)
                out.append(x)
            return tuple(out)

        none = jnp.zeros((STEP, ROWS), jnp.float32)
        packed = lax.fori_loop(0, STEPS, pack, (none, none))
        for a in range(2):
            pk[c, a] = packed[a]
        for way, to in enumerate((after, before)):
            copy = pltpu.make_async_remote_copy(
                src_ref=pk.at[c], dst_ref=pkr.at[c, way], send_sem=psend.at[c, way], recv_sem=precv.at[c, way],
                device_id=(to, lon), device_id_type=MESH,
            )
            copy.start()
            lat_copies.append(copy)

    for copy in nest_copies:
        copy.wait_recv()
    for n in range(12):
        nasm[n // 6, n % 6] = jnp.concatenate([ngat[d, n : n + 1, :] for d in range(SEGS)], axis=0)
    spread = []
    eight = pl.ds(pl.multiple_of(lat * SEGS, SEGS), SEGS)
    for k in range(1, BANDS):
        to = lax.rem(lat + k, BANDS)
        copy = pltpu.make_async_remote_copy(
            src_ref=nasm.at[to // (BANDS // 2)], dst_ref=nestg.at[:, eight, :], send_sem=n2s.at[k],
            recv_sem=n2r.at[k], device_id=(to, lon), device_id_type=MESH,
        )
        copy.start()
        spread.append(copy)
    own_nest = pltpu.make_async_copy(nasm.at[lat // (BANDS // 2)], nestg.at[:, eight, :], osem.at[LEV])
    own_nest.start()

    for copy in lon_copies:
        copy.wait_recv()
    edge_row = rc[lat, 0:1, :]
    inverse_cos = rc[lat, 1:2, :]
    first_edge, last_edge = rc[lat, 2:3, :], rc[lat, 3:4, :]
    flux_scale = jnp.where(even[:1], last_edge, first_edge)

    def fluxes(c, put):
        for copy in loads[c][2:]:
            copy.wait()
        for way in range(2):
            lat_copies[2 * c + way].wait_recv()
        sums = [
            pk[c, a] + jnp.where(even, pltpu.roll(pkr[c, 1, a], ROWS - 1, 1), pltpu.roll(pkr[c, 0, a], 1, 1))
            for a in range(2)
        ]
        fl[c] = sums[0] * sums[1] * flux_scale
        for h in range(PAIR):
            lev = PAIR * c + h
            tb[lev, SEG : SEG + 1, :] = lh[0, 0, lev]
            zb[lev, SEG : SEG + 1, :] = lh[1, 0, lev]
            west = 0.0625 * (lh[1, 1, lev] + zb[lev, 0:1, :]) * (lh[0, 1, lev] + tb[lev, 0:1, :])

            def step(b, west, lev=lev, h=h):
                r = pl.multiple_of(b * STEP, STEP)
                t_all = tb[lev, pl.ds(r, STEP + 8), :]
                z_all = zb[lev, pl.ds(r, STEP + 8), :]
                t = t_all[:STEP]
                east = 0.0625 * (z_all[:STEP] + z_all[1 : STEP + 1]) * (t + t_all[1 : STEP + 1])
                zonal = east - jnp.concatenate([west, east[: STEP - 1]], axis=0)
                m = mb[lev, pl.ds(r, STEP), :]
                ends = pltpu.roll(fl[c], lax.rem(2 * ROWS - 1 - 4 * b - 2 * h, ROWS), 1)
                south = edge_row * (t + pltpu.roll(t, ROWS - 1, 1)) * (m + pltpu.roll(m, ROWS - 1, 1))
                south = jnp.where(lane == ROWS - 1, ends, south)
                north = jnp.where(lane == 0, ends, pltpu.roll(south, 1, 1))
                s = sb[lev, pl.ds(r, STEP), :]
                put(lev, h, r, 0.75 * s + 0.25 * t - zonal - inverse_cos * (south - north))
                return east[STEP - 1 : STEP]

            lax.fori_loop(0, STEPS, step, west)

    @pl.when(jnp.logical_not(polar))
    def _():
        def put(lev, h, r, value):
            sb[lev, pl.ds(r, STEP), :] = value

        outs = []
        for c in range(CHUNKS):
            fluxes(c, put)
            pair = pl.ds(PAIR * c, PAIR)
            copy = pltpu.make_async_copy(sb.at[pair, pl.ds(0, SEG)], sect.at[pair], osem.at[c])
            copy.start()
            outs.append(copy)
        for copy in outs:
            copy.wait()
        for copy in tables:
            copy.wait()

    @pl.when(polar)
    def _():
        def put(lev, h, r, value):
            hi, lo = hi_lo(value)
            sh[pl.ds(r, STEP), h * ROWS : (h + 1) * ROWS] = hi
            sl[pl.ds(r, STEP), h * ROWS : (h + 1) * ROWS] = lo

        block = lanes((PART, ROWS)) // 32

        def exchange(c, k, src, dst, send, receive):
            return pltpu.make_async_remote_copy(
                src_ref=src.at[c, lax.rem(lon + k, SEGS)], dst_ref=dst.at[c, lon], send_sem=send.at[c, k],
                recv_sem=receive.at[c, k], device_id=(lat, lax.rem(lon + k, SEGS)), device_id_type=MESH,
            )

        there = []
        for c in range(CHUNKS):
            fluxes(c, put)
            if c == 0:
                tables[0].wait()
            both = dot(ut[...], sh[...])
            y = both[:RANK] + both[RANK:] + dot(ut[:RANK, :], sl[...])
            for h in range(PAIR):
                for q in range(4):
                    acc = None
                    for j in range(4):
                        v = y[PART * j : PART * (j + 1), ROWS * h : ROWS * (h + 1)]
                        if j != q:
                            v = pltpu.roll(v, (32 * (j - q)) % ROWS, 1)
                        acc = v if acc is None else jnp.where(block == j, v, acc)
                    fsend[c, 4 * h + q] = acc
            recv[c, lon] = fsend[c, lon]
            there.append([exchange(c, k, fsend, recv, fs, fr) for k in range(1, SEGS)])
            for copy in there[c]:
                copy.start()

        tables[1].wait()
        tables[2].wait()
        rows_cut = pltpu.roll(jnp.broadcast_to(cut[pl.ds(lat, 1), :], (8, ROWS)), ROWS - 32 * lax.rem(lon, 4), 1)[:1]
        n = lax.broadcasted_iota(jnp.int32, (256, ROWS), 0)
        root = math.sqrt(0.5)
        back, own = [], []
        for c in range(CHUNKS):
            for copy in there[c]:
                copy.wait_recv()
            y = [recv[c, d] for d in range(SEGS)]
            u = [y[j] + y[j + 4] for j in range(4)]
            v = [y[j] - y[j + 4] for j in range(4)]
            a, b, m, p = u[0] + u[2], u[1] + u[3], root * (v[1] - v[3]), root * (v[1] + v[3])
            groups = [(a + b, a - b), (v[0] + m, -v[2] - p), (u[0] - u[2], u[3] - u[1]), (v[0] - m, v[2] - p)]
            spectra = []
            for g, two in enumerate(groups):
                tall = jnp.concatenate(
                    [x if j == 0 else pltpu.roll(x, ROWS - 32 * j, 1) for x in two for j in range(4)], axis=0
                )
                hi, lo = hi_lo(tall)
                rhs = jnp.concatenate([hi, lo, hi, jnp.zeros((WIDE - 960, ROWS), jnp.bfloat16)], axis=0)
                wave = dot(pt[g], rhs)
                number = 8 * (n & 63) + jnp.where((n & 64) == 0, g, 4 if g == 0 else 8 - g)
                wave = jnp.where(number <= rows_cut, wave, 0.0)
                hi, lo = hi_lo(wave)
                full = dot(qt[g], jnp.concatenate([hi, lo, hi], axis=0))
                for x in range(2):
                    acc = None
                    for j in range(4):
                        w = full[RANK * x + PART * j : RANK * x + PART * (j + 1)]
                        if j:
                            w = pltpu.roll(w, 32 * j, 1)
                        acc = w if acc is None else jnp.where(block == j, w, acc)
                    spectra.append(acc)
            w0, w4, r1, i1, r2, i2, r3, i3 = spectra
            plus, minus = w0 + w4, w0 - w4
            evens = [plus + r2, minus - i2, plus - r2, minus + i2]
            d1, d2 = root * (r1 - r3), root * (i1 + i3)
            odds = [r1 + r3, d1 - d2, i3 - i1, -d1 - d2]
            for e in range(4):
                bsend[c, e] = evens[e] + odds[e]
                bsend[c, e + 4] = evens[e] - odds[e]
            back.append([exchange(c, k, bsend, zout, bs, br) for k in range(1, SEGS)])
            for copy in back[c]:
                copy.start()
            copy = pltpu.make_async_copy(bsend.at[c, lon], zout.at[c, lon], zsem.at[c])
            copy.start()
            own.append(copy)
        for c in range(CHUNKS):
            own[c].wait()
            for copy in back[c]:
                copy.wait_recv()
        for c in range(CHUNKS):
            for copy in there[c] + back[c]:
                copy.wait_send()

    for copy in spread:
        copy.wait_recv()
    own_nest.wait()
    for copy in lon_copies + nest_copies + lat_copies + spread:
        copy.wait_send()


def finish_kernel(lat_ref, corners, zin, eu, sect, nestg, out, ob, nb, zc, osem, nsem):
    lat, lon = lat_ref[0], lat_ref[1]
    polar = (lat < BANDS // 4) | (lat >= BANDS - BANDS // 4)
    half = lat // (BANDS // 2)
    row = corners[half, 0] - lat * ROWS
    col = corners[half, 1] - lon * SEG
    hit = (row > -ROWS) & (row < ROWS) & (col > -256) & (col < SEG)
    fetch = pltpu.make_async_copy(nestg, nb, nsem)

    @pl.when(hit)
    def _():
        fetch.start()

    @pl.when(jnp.logical_not(polar))
    def _():
        copy = pltpu.make_async_copy(sect, ob.at[:, pl.ds(256, SEG), :], osem.at[0])
        copy.start()
        copy.wait()

    block = lanes((PART, ROWS)) // 32

    @pl.when(polar)
    def _():
        for c in range(CHUNKS):
            for h in range(PAIR):
                for j in range(4):
                    acc = None
                    for q in range(4):
                        v = zin[c, 4 * h + q]
                        if j != q:
                            v = pltpu.roll(v, (32 * (q - j)) % ROWS, 1)
                        acc = v if acc is None else jnp.where(block == q, v, acc)
                    zc[PART * j : PART * (j + 1), h * ROWS : (h + 1) * ROWS] = acc
            hi, lo = hi_lo(zc[...])
            rhs = jnp.concatenate([hi, lo, hi, jnp.zeros((32, 2 * ROWS), jnp.bfloat16)], axis=0)
            full = dot(eu[...], rhs)
            for h in range(PAIR):
                ob[PAIR * c + h, 256 : 256 + STEP * STEPS, :] = full[:, h * ROWS : (h + 1) * ROWS]

    @pl.when(hit)
    def _():
        fetch.wait()
        lane = lanes((264, ROWS))
        cell = lax.broadcasted_iota(jnp.int32, (264, ROWS), 0)
        place = col + 256
        base = pl.multiple_of((place // 8) * 8, 8)
        off = place - base
        inside = (lane >= row) & (lane < row + ROWS) & (cell >= off) & (cell < off + 256)
        for lev in range(LEV):
            flat = jnp.swapaxes(nb[lev], 0, 1)
            tall = jnp.concatenate([flat, jnp.zeros((8, ROWS), jnp.float32)], axis=0)
            tall = pltpu.roll(pltpu.roll(tall, off, 0), lax.rem(row + ROWS, ROWS), 1)
            here = ob[lev, pl.ds(base, 264), :]
            ob[lev, pl.ds(base, 264), :] = jnp.where(inside, tall, here)

    copies = []
    for lev in range(LEV):
        copy = pltpu.make_async_copy(ob.at[lev, pl.ds(256, SEG), :], out.at[lev], osem.at[lev])
        copy.start()
        copies.append(copy)
    for copy in copies:
        copy.wait()


def shards(start, sec, zon, mer, cutoffs, nest_values, nest_corners, tables):
    ut, eu, pt, qt, rc = (jnp.asarray(x) for x in tables)
    flip = lambda x: jnp.swapaxes(x, 1, 2)
    anywhere = pl.BlockSpec(memory_space=pl.ANY)
    vmem = pl.BlockSpec(memory_space=pltpu.VMEM)
    smem = pl.BlockSpec(memory_space=pltpu.SMEM)
    f32, bf = jnp.float32, jnp.bfloat16
    dma = pltpu.SemaphoreType.DMA
    field = pltpu.VMEM((LEV, TALL, ROWS), f32)
    zout, sect, nestg = pl.pallas_call(
        section_kernel,
        out_shape=(
            jax.ShapeDtypeStruct((CHUNKS, SEGS, PART, ROWS), f32),
            jax.ShapeDtypeStruct((LEV, SEG, ROWS), f32),
            jax.ShapeDtypeStruct((LEV, 128, 256), f32),
        ),
        in_specs=[anywhere] * 7 + [vmem] * 3,
        out_specs=(anywhere,) * 3,
        scratch_shapes=[
            field, field, field, field,
            pltpu.VMEM((2 * RANK, WIDE), bf), pltpu.VMEM((4, 256, WIDE), bf), pltpu.VMEM((4, 2 * RANK, 768), bf),
            pltpu.VMEM((WIDE, 256), bf), pltpu.VMEM((WIDE, 256), bf),
            pltpu.VMEM((CHUNKS, 2, STEP, ROWS), f32), pltpu.VMEM((CHUNKS, 2, 2, STEP, ROWS), f32),
            pltpu.VMEM((CHUNKS, STEP, ROWS), f32), pltpu.VMEM((2, 2, LEV, 1, ROWS), f32),
            pltpu.VMEM((CHUNKS, SEGS, PART, ROWS), f32), pltpu.VMEM((CHUNKS, SEGS, PART, ROWS), f32),
            pltpu.VMEM((CHUNKS, SEGS, PART, ROWS), f32),
            pltpu.VMEM((16, 256), f32), pltpu.VMEM((SEGS, 16, 256), f32), pltpu.VMEM((2, LEV, SEGS, 256), f32),
            dma((CHUNKS, 4)), dma((3,)), dma((CHUNKS, 2)), dma((CHUNKS, 2)), dma((2, 2)), dma((2, 2)),
            dma((CHUNKS, SEGS)), dma((CHUNKS, SEGS)), dma((CHUNKS, SEGS)), dma((CHUNKS, SEGS)),
            dma((SEGS,)), dma((SEGS,)), dma((BANDS,)), dma((BANDS,)), dma((LEV + 1,)), dma((CHUNKS,)),
        ],
        compiler_params=pltpu.CompilerParams(
            collective_id=0, has_side_effects=True, vmem_limit_bytes=56 * 2**20
        ),
        cost_estimate=pl.CostEstimate(flops=10**9, bytes_accessed=16 * 10**6, transcendentals=0),
    )(
        flip(start), flip(sec), flip(zon), flip(mer), ut, pt, qt,
        cutoffs.reshape(BANDS, ROWS), rc, nest_values,
    )
    where = jnp.stack([lax.axis_index("lat"), lax.axis_index("lon")]).astype(jnp.int32)
    result = pl.pallas_call(
        finish_kernel,
        out_shape=jax.ShapeDtypeStruct((LEV, SEG, ROWS), f32),
        in_specs=[smem, smem, vmem, vmem, anywhere, anywhere],
        out_specs=anywhere,
        scratch_shapes=[
            pltpu.VMEM((LEV, 256 + 928 + 256, ROWS), f32),
            pltpu.VMEM((LEV, 128, 256), f32),
            pltpu.VMEM((RANK, 2 * ROWS), f32),
            dma((LEV,)),
            dma,
        ],
        compiler_params=pltpu.CompilerParams(vmem_limit_bytes=56 * 2**20),
        cost_estimate=pl.CostEstimate(flops=10**9, bytes_accessed=4 * 10**6, transcendentals=0),
    )(where, nest_corners, zout, eu, sect, nestg)
    return flip(result)


def solution(mesh):
    tables = make_tables()
    spec = P(None, "lat", "lon")
    return jax.shard_map(
        lambda *args: shards(*args, tables),
        mesh=mesh,
        in_specs=(spec, spec, spec, spec, P(), P(None, None, ("lat", "lon"), None), P()),
        out_specs=spec,
        check_vma=False,
    )
```

```python
import math

import jax
import jax.numpy as jnp
import ml_dtypes
import numpy as np
from jax import lax
from jax.experimental import pallas as pl
from jax.experimental.pallas import tpu as pltpu
from jax.sharding import PartitionSpec as P

LEV, NLAT, NLON, KMAX = 6, 2048, 7200, 512
BANDS, SEGS = 16, 8
ROWS, SEG = NLAT // BANDS, NLON // SEGS
RANK = 160
PART = RANK // 4
CHUNKS, PAIR = 3, 2
STEP, STEPS = 32, 29
CELLS = STEP * STEPS
TALL = CELLS + 8
WIDE = 1024
MESH = pl.DeviceIdType.MESH
BF = ml_dtypes.bfloat16


def tri_solve(diag, off, shift, rhs):
    n, r = rhs.shape
    b = rhs.copy()
    d, u1, u2 = (np.zeros((n, r)) for _ in range(3))
    cd, cu, cb = diag[0] - shift, np.full(r, off[0]), b[0]
    for j in range(n - 1):
        nd, nu, sub = diag[j + 1] - shift, off[j + 1] if j + 2 < n else 0.0, off[j]
        swap = np.abs(sub) > np.abs(cd)
        p = np.where(swap, sub, np.where(cd == 0, 1e-30, cd))
        pu1, pu2, pb = np.where(swap, nd, cu), np.where(swap, nu, 0.0), np.where(swap, b[j + 1], cb)
        o, ou1 = np.where(swap, cd, sub), np.where(swap, cu, nd)
        ou2, ob = np.where(swap, 0.0, nu), np.where(swap, cb, b[j + 1])
        f = o / p
        d[j], u1[j], u2[j], b[j] = p, pu1, pu2, pb
        cd, cu, cb = ou1 - f * pu1, ou2 - f * pu2, ob - f * pb
    d[n - 1] = np.where(np.abs(cd) < 1e-20, 1e-20, cd)
    b[n - 1] = cb
    x = np.zeros((n, r))
    x[n - 1] = b[n - 1] / d[n - 1]
    x[n - 2] = (b[n - 2] - u1[n - 2] * x[n - 1]) / d[n - 2]
    for j in range(n - 3, -1, -1):
        x[j] = (b[j] - u1[j] * x[j + 1] - u2[j] * x[j + 2]) / d[j]
    return x


def slepian(length, width, rank):
    i = np.arange(length, dtype=np.float64)
    diag = ((length - 1 - 2 * i) / 2) ** 2 * np.cos(2 * np.pi * width)
    off = (i * (length - i) / 2)[1:]
    off2 = np.concatenate([[0.0], off**2])
    bound = np.abs(diag).max() + 2 * off.max()
    low, high, want = np.full(rank, -bound), np.full(rank, bound), np.arange(rank)
    for _ in range(70):
        mid = 0.5 * (low + high)
        above, q = np.zeros(rank, dtype=np.int64), np.ones(rank)
        for j in range(length):
            q = diag[j] - mid - off2[j] / q
            q = np.where(q == 0.0, 1e-300, q)
            above += q > 0
        up = above > want
        low, high = np.where(up, mid, low), np.where(up, high, mid)
    x = np.ones((length, rank)) + 0.3 * np.cos(i * i)[:, None]
    for _ in range(4):
        x = tri_solve(diag, off, 0.5 * (low + high), x)
        x = x / np.sqrt((x * x).sum(0))
    return x


def split(x):
    hi = x.astype(BF)
    return hi, (x - hi.astype(np.float64)).astype(BF)


def make_tables():
    basis = slepian(SEG, 512.0 / NLON, RANK)
    k, i = np.arange(KMAX), np.arange(SEG)
    waves = np.exp(-2j * np.pi * ((i[:, None] * k[None, :]) % NLON) / NLON)
    v = np.einsum("ir,ik->rk", basis, waves)
    weight = np.where(k == 0, 1.0, 2.0) / NLON
    uh, ul = split(basis)
    ut = np.zeros((2 * RANK, WIDE), BF)
    ut[:RANK, :SEG], ut[RANK:, :SEG] = uh.T, ul.T
    eu = np.zeros((CELLS, 512), BF)
    eu[:SEG, :RANK], eu[:SEG, RANK : 2 * RANK], eu[:SEG, 2 * RANK : 3 * RANK] = uh, uh, ul
    pt = np.zeros((4, 256, WIDE), BF)
    qt = np.zeros((4, 2 * RANK, 768), BF)
    for g in range(4):
        s1, s2 = g, (4 if g == 0 else 8 - g)
        k1, k2 = np.arange(64) * 8 + s1, np.arange(64) * 8 + s2
        v1, v2 = v[:, k1], v[:, k2]
        w1, w2 = weight[k1], weight[k2]
        z = np.zeros((RANK, 64))
        if g == 0:
            p = np.block([[v1.real, z, v1.imag, z], [z, v2.real, z, v2.imag]])
            q = np.block([[v1.real * w1, z, v1.imag * w1, z], [z, v2.real * w2, z, v2.imag * w2]])
        else:
            p = np.block([[v1.real, v2.real, v1.imag, v2.imag], [-v1.imag, v2.imag, v1.real, -v2.real]])
            q = np.block(
                [
                    [v1.real * w1, v2.real * w2, v1.imag * w1, v2.imag * w2],
                    [-v1.imag * w1, v2.imag * w2, v1.real * w1, -v2.real * w2],
                ]
            )
        ph, pl_ = split(p.T)
        pt[g, :, :320], pt[g, :, 320:640], pt[g, :, 640:960] = ph, ph, pl_
        qh, ql = split(q)
        qt[g, :, :256], qt[g, :, 256:512], qt[g, :, 512:] = qh, qh, ql
    step = np.float32(math.pi / NLAT)
    half = np.float32(math.pi / 2)
    e = np.arange(NLAT + 1)
    edge = np.cos((e.astype(np.float32) * step - half).astype(np.float64)).astype(np.float32)
    edge[0] = edge[-1] = 0.0
    center = np.cos(((np.arange(NLAT).astype(np.float32) + np.float32(0.5)) * step - half).astype(np.float64))
    rc = np.zeros((BANDS, 8, ROWS), np.float32)
    for b in range(BANDS):
        r0 = b * ROWS
        rc[b, 0] = 0.0625 * edge[r0 + 1 : r0 + ROWS + 1]
        rc[b, 1] = (1.0 / center[r0 : r0 + ROWS]).astype(np.float32)
        rc[b, 2] = 0.0625 * edge[r0]
        rc[b, 3] = 0.0625 * edge[r0 + ROWS]
    return ut, eu, pt, qt, rc


def lanes(shape):
    return lax.broadcasted_iota(jnp.int32, shape, len(shape) - 1)


def hi_lo(x):
    hi = x.astype(jnp.bfloat16)
    return hi, (x - hi.astype(jnp.float32)).astype(jnp.bfloat16)


def dot(a, b):
    return jnp.dot(a, b, preferred_element_type=jnp.float32)


def section_kernel(
    start, sec, zon, mer, ut_h, pt_h, qt_h, cut, rc, nest,
    zout, sect, nestg,
    sb, tb, zb, mb, ut, pt, qt, sh, sl, pk, pkr, fl, lh,
    fsend, recv, bsend, nsend, ngat, nasm,
    ld, tabs, psend, precv, lsend, lrecv, fs, fr, bs, br, n1s, n1r, n2s, n2r, osem, zsem,
):
    lat, lon = lax.axis_index("lat"), lax.axis_index("lon")
    polar = (lat < BANDS // 4) | (lat >= BANDS - BANDS // 4)

    loads = []
    for c in range(CHUNKS):
        pair = pl.ds(PAIR * c, PAIR)
        loads.append([])
        for a, (src, dst) in enumerate(((sec, tb), (mer, mb), (zon, zb), (start, sb))):
            copy = pltpu.make_async_copy(src.at[pair], dst.at[pair, pl.ds(0, SEG)], ld.at[c, a])
            copy.start()
            loads[c].append(copy)
    tables = [
        pltpu.make_async_copy(src, dst, tabs.at[n]) for n, (src, dst) in enumerate(((ut_h, ut), (pt_h, pt), (qt_h, qt)))
    ]
    for copy in tables:
        copy.start()

    barrier = pltpu.get_barrier_semaphore()
    for k in range(1, SEGS):
        pl.semaphore_signal(barrier, inc=1, device_id=(lat, lax.rem(lon + k, SEGS)), device_id_type=MESH)
    for k in range(1, BANDS):
        pl.semaphore_signal(barrier, inc=1, device_id=(lax.rem(lat + k, BANDS), lon), device_id_type=MESH)
    for n in range(12):
        nsend[n : n + 1, :] = nest[n // 6, n % 6]
    nsend[12:16, :] = jnp.zeros((4, 256), jnp.float32)
    for buf in (tb, zb, mb, sb):
        for lev in range(LEV):
            buf[lev, SEG:TALL, :] = jnp.zeros((TALL - SEG, ROWS), jnp.float32)
    sh[CELLS :, :] = jnp.zeros((WIDE - CELLS, 256), jnp.bfloat16)
    sl[CELLS :, :] = jnp.zeros((WIDE - CELLS, 256), jnp.bfloat16)
    pl.semaphore_wait(barrier, SEGS - 1 + BANDS - 1)

    left, right = lax.rem(lon + SEGS - 1, SEGS), lax.rem(lon + 1, SEGS)
    lon_copies = []
    for a, src in enumerate((sec, zon)):
        for way, (row, to) in enumerate(((0, left), (SEG - 1, right))):
            copy = pltpu.make_async_remote_copy(
                src_ref=src.at[:, pl.ds(row, 1), :], dst_ref=lh.at[a, way], send_sem=lsend.at[a, way],
                recv_sem=lrecv.at[a, way], device_id=(lat, to), device_id_type=MESH,
            )
            copy.start()
            lon_copies.append(copy)
    nest_copies = []
    for k in range(1, SEGS):
        copy = pltpu.make_async_remote_copy(
            src_ref=nsend, dst_ref=ngat.at[lon], send_sem=n1s.at[k], recv_sem=n1r.at[k],
            device_id=(lat, lax.rem(lon + k, SEGS)), device_id_type=MESH,
        )
        copy.start()
        nest_copies.append(copy)
    ngat[lon] = nsend[...]

    before, after = lax.rem(lat + BANDS - 1, BANDS), lax.rem(lat + 1, BANDS)
    lane = lanes((STEP, ROWS))
    even = (lane & 1) == 0
    lat_copies = []
    for c in range(CHUNKS):
        loads[c][0].wait()
        loads[c][1].wait()

        def pack(b, acc, c=c):
            out = []
            for buf, x in zip((tb, mb), acc):
                for h in range(PAIR):
                    v = buf[PAIR * c + h, pl.ds(pl.multiple_of(b * STEP, STEP), STEP), :]
                    x = jnp.where((lane >> 1) == 2 * b + h, pltpu.roll(v, lax.rem(4 * b + 2 * h + 1, ROWS), 1), x)
                out.append(x)
            return tuple(out)

        none = jnp.zeros((STEP, ROWS), jnp.float32)
        packed = lax.fori_loop(0, STEPS, pack, (none, none), unroll=True)
        for a in range(2):
            pk[c, a] = packed[a]
        for way, to in enumerate((after, before)):
            copy = pltpu.make_async_remote_copy(
                src_ref=pk.at[c], dst_ref=pkr.at[c, way], send_sem=psend.at[c, way], recv_sem=precv.at[c, way],
                device_id=(to, lon), device_id_type=MESH,
            )
            copy.start()
            lat_copies.append(copy)

    for copy in nest_copies:
        copy.wait_recv()
    for n in range(12):
        nasm[n // 6, n % 6] = jnp.concatenate([ngat[d, n : n + 1, :] for d in range(SEGS)], axis=0)
    spread = []
    eight = pl.ds(pl.multiple_of(lat * SEGS, SEGS), SEGS)
    for k in range(1, BANDS):
        to = lax.rem(lat + k, BANDS)
        copy = pltpu.make_async_remote_copy(
            src_ref=nasm.at[to // (BANDS // 2)], dst_ref=nestg.at[:, eight, :], send_sem=n2s.at[k],
            recv_sem=n2r.at[k], device_id=(to, lon), device_id_type=MESH,
        )
        copy.start()
        spread.append(copy)
    own_nest = pltpu.make_async_copy(nasm.at[lat // (BANDS // 2)], nestg.at[:, eight, :], osem.at[LEV])
    own_nest.start()

    for copy in lon_copies:
        copy.wait_recv()
    edge_row = rc[lat, 0:1, :]
    inverse_cos = rc[lat, 1:2, :]
    first_edge, last_edge = rc[lat, 2:3, :], rc[lat, 3:4, :]
    tall_lane = lanes((CELLS, ROWS))
    flux_scale = jnp.where(even[:1], last_edge, first_edge)

    def fluxes(c, put):
        for copy in loads[c][2:]:
            copy.wait()
        for way in range(2):
            lat_copies[2 * c + way].wait_recv()
        sums = [
            pk[c, a] + jnp.where(even, pltpu.roll(pkr[c, 1, a], ROWS - 1, 1), pltpu.roll(pkr[c, 0, a], 1, 1))
            for a in range(2)
        ]
        fl[c] = sums[0] * sums[1] * flux_scale
        for h in range(PAIR):
            lev = PAIR * c + h
            tb[lev, SEG : SEG + 1, :] = lh[0, 0, lev]
            zb[lev, SEG : SEG + 1, :] = lh[1, 0, lev]
            west = 0.0625 * (lh[1, 1, lev] + zb[lev, 0:1, :]) * (lh[0, 1, lev] + tb[lev, 0:1, :])

            t_all, z_all = tb[lev], zb[lev]
            t = t_all[:CELLS]
            east = 0.0625 * (z_all[:CELLS] + z_all[1 : CELLS + 1]) * (t + t_all[1 : CELLS + 1])
            zonal = east - jnp.concatenate([west, east[: CELLS - 1]], axis=0)
            m = mb[lev, :CELLS, :]
            packed = fl[c]
            ends = jnp.concatenate(
                [pltpu.roll(packed, (2 * ROWS - 1 - 4 * b - 2 * h) % ROWS, 1) for b in range(STEPS)], axis=0
            )
            south = edge_row * (t + pltpu.roll(t, ROWS - 1, 1)) * (m + pltpu.roll(m, ROWS - 1, 1))
            south = jnp.where(tall_lane == ROWS - 1, ends, south)
            north = jnp.where(tall_lane == 0, ends, pltpu.roll(south, 1, 1))
            put(lev, h, 0.75 * sb[lev, :CELLS, :] + 0.25 * t - zonal - inverse_cos * (south - north))

    @pl.when(jnp.logical_not(polar))
    def _():
        def put(lev, h, value):
            sb[lev, :CELLS, :] = value

        outs = []
        for c in range(CHUNKS):
            fluxes(c, put)
            pair = pl.ds(PAIR * c, PAIR)
            copy = pltpu.make_async_copy(sb.at[pair, pl.ds(0, SEG)], sect.at[pair], osem.at[c])
            copy.start()
            outs.append(copy)
        for copy in outs:
            copy.wait()
        for copy in tables:
            copy.wait()

    @pl.when(polar)
    def _():
        def put(lev, h, value):
            hi, lo = hi_lo(value)
            sh[:CELLS, h * ROWS : (h + 1) * ROWS] = hi
            sl[:CELLS, h * ROWS : (h + 1) * ROWS] = lo

        block = lanes((PART, ROWS)) // 32

        def exchange(c, k, src, dst, send, receive):
            return pltpu.make_async_remote_copy(
                src_ref=src.at[c, lax.rem(lon + k, SEGS)], dst_ref=dst.at[c, lon], send_sem=send.at[c, k],
                recv_sem=receive.at[c, k], device_id=(lat, lax.rem(lon + k, SEGS)), device_id_type=MESH,
            )

        there = []
        for c in range(CHUNKS):
            fluxes(c, put)
            if c == 0:
                tables[0].wait()
            both = dot(ut[...], sh[...])
            y = both[:RANK] + both[RANK:] + dot(ut[:RANK, :], sl[...])
            for h in range(PAIR):
                for q in range(4):
                    acc = None
                    for j in range(4):
                        v = y[PART * j : PART * (j + 1), ROWS * h : ROWS * (h + 1)]
                        if j != q:
                            v = pltpu.roll(v, (32 * (j - q)) % ROWS, 1)
                        acc = v if acc is None else jnp.where(block == j, v, acc)
                    fsend[c, 4 * h + q] = acc
            recv[c, lon] = fsend[c, lon]
            there.append([exchange(c, k, fsend, recv, fs, fr) for k in range(1, SEGS)])
            for copy in there[c]:
                copy.start()

        tables[1].wait()
        tables[2].wait()
        rows_cut = pltpu.roll(jnp.broadcast_to(cut[pl.ds(lat, 1), :], (8, ROWS)), ROWS - 32 * lax.rem(lon, 4), 1)[:1]
        n = lax.broadcasted_iota(jnp.int32, (256, ROWS), 0)
        root = math.sqrt(0.5)
        back, own = [], []
        for c in range(CHUNKS):
            for copy in there[c]:
                copy.wait_recv()
            y = [recv[c, d] for d in range(SEGS)]
            u = [y[j] + y[j + 4] for j in range(4)]
            v = [y[j] - y[j + 4] for j in range(4)]
            a, b, m, p = u[0] + u[2], u[1] + u[3], root * (v[1] - v[3]), root * (v[1] + v[3])
            groups = [(a + b, a - b), (v[0] + m, -v[2] - p), (u[0] - u[2], u[3] - u[1]), (v[0] - m, v[2] - p)]
            spectra = []
            for g, two in enumerate(groups):
                tall = jnp.concatenate(
                    [x if j == 0 else pltpu.roll(x, ROWS - 32 * j, 1) for x in two for j in range(4)], axis=0
                )
                hi, lo = hi_lo(tall)
                rhs = jnp.concatenate([hi, lo, hi, jnp.zeros((WIDE - 960, ROWS), jnp.bfloat16)], axis=0)
                wave = dot(pt[g], rhs)
                number = 8 * (n & 63) + jnp.where((n & 64) == 0, g, 4 if g == 0 else 8 - g)
                wave = jnp.where(number <= rows_cut, wave, 0.0)
                hi, lo = hi_lo(wave)
                full = dot(qt[g], jnp.concatenate([hi, lo, hi], axis=0))
                for x in range(2):
                    acc = None
                    for j in range(4):
                        w = full[RANK * x + PART * j : RANK * x + PART * (j + 1)]
                        if j:
                            w = pltpu.roll(w, 32 * j, 1)
                        acc = w if acc is None else jnp.where(block == j, w, acc)
                    spectra.append(acc)
            w0, w4, r1, i1, r2, i2, r3, i3 = spectra
            plus, minus = w0 + w4, w0 - w4
            evens = [plus + r2, minus - i2, plus - r2, minus + i2]
            d1, d2 = root * (r1 - r3), root * (i1 + i3)
            odds = [r1 + r3, d1 - d2, i3 - i1, -d1 - d2]
            for e in range(4):
                bsend[c, e] = evens[e] + odds[e]
                bsend[c, e + 4] = evens[e] - odds[e]
            back.append([exchange(c, k, bsend, zout, bs, br) for k in range(1, SEGS)])
            for copy in back[c]:
                copy.start()
            copy = pltpu.make_async_copy(bsend.at[c, lon], zout.at[c, lon], zsem.at[c])
            copy.start()
            own.append(copy)
        for c in range(CHUNKS):
            own[c].wait()
            for copy in back[c]:
                copy.wait_recv()
        for c in range(CHUNKS):
            for copy in there[c] + back[c]:
                copy.wait_send()

    for copy in spread:
        copy.wait_recv()
    own_nest.wait()
    for copy in lon_copies + nest_copies + lat_copies + spread:
        copy.wait_send()


def finish_kernel(corners, zin, eu, sect, nestg, out, ob, nb, zc, osem, nsem):
    lat, lon = lax.axis_index("lat"), lax.axis_index("lon")
    polar = (lat < BANDS // 4) | (lat >= BANDS - BANDS // 4)
    half = lat // (BANDS // 2)
    row = corners[half, 0] - lat * ROWS
    col = corners[half, 1] - lon * SEG
    hit = (row > -ROWS) & (row < ROWS) & (col > -256) & (col < SEG)
    fetch = pltpu.make_async_copy(nestg, nb, nsem)

    @pl.when(hit)
    def _():
        fetch.start()

    @pl.when(jnp.logical_not(polar))
    def _():
        copy = pltpu.make_async_copy(sect, ob.at[:, pl.ds(256, SEG), :], osem.at[0])
        copy.start()
        copy.wait()

    block = lanes((PART, ROWS)) // 32

    @pl.when(polar)
    def _():
        for c in range(CHUNKS):
            for h in range(PAIR):
                for j in range(4):
                    acc = None
                    for q in range(4):
                        v = zin[c, 4 * h + q]
                        if j != q:
                            v = pltpu.roll(v, (32 * (q - j)) % ROWS, 1)
                        acc = v if acc is None else jnp.where(block == q, v, acc)
                    zc[PART * j : PART * (j + 1), h * ROWS : (h + 1) * ROWS] = acc
            hi, lo = hi_lo(zc[...])
            rhs = jnp.concatenate([hi, lo, hi, jnp.zeros((32, 2 * ROWS), jnp.bfloat16)], axis=0)
            full = dot(eu[...], rhs)
            for h in range(PAIR):
                ob[PAIR * c + h, 256 : 256 + CELLS, :] = full[:, h * ROWS : (h + 1) * ROWS]

    @pl.when(hit)
    def _():
        fetch.wait()
        lane = lanes((264, ROWS))
        cell = lax.broadcasted_iota(jnp.int32, (264, ROWS), 0)
        place = col + 256
        base = pl.multiple_of((place // 8) * 8, 8)
        off = place - base
        inside = (lane >= row) & (lane < row + ROWS) & (cell >= off) & (cell < off + 256)
        for lev in range(LEV):
            flat = jnp.swapaxes(nb[lev], 0, 1)
            tall = jnp.concatenate([flat, jnp.zeros((8, ROWS), jnp.float32)], axis=0)
            tall = pltpu.roll(pltpu.roll(tall, off, 0), lax.rem(row + ROWS, ROWS), 1)
            here = ob[lev, pl.ds(base, 264), :]
            ob[lev, pl.ds(base, 264), :] = jnp.where(inside, tall, here)

    copies = []
    for lev in range(LEV):
        copy = pltpu.make_async_copy(ob.at[lev, pl.ds(256, SEG), :], out.at[lev], osem.at[lev])
        copy.start()
        copies.append(copy)
    for copy in copies:
        copy.wait()


def shards(start, sec, zon, mer, cutoffs, nest_values, nest_corners, tables):
    ut, eu, pt, qt, rc = (jnp.asarray(x) for x in tables)
    flip = lambda x: jnp.swapaxes(x, 1, 2)
    anywhere = pl.BlockSpec(memory_space=pl.ANY)
    vmem = pl.BlockSpec(memory_space=pltpu.VMEM)
    smem = pl.BlockSpec(memory_space=pltpu.SMEM)
    f32, bf = jnp.float32, jnp.bfloat16
    dma = pltpu.SemaphoreType.DMA
    field = pltpu.VMEM((LEV, TALL, ROWS), f32)
    zout, sect, nestg = pl.pallas_call(
        section_kernel,
        out_shape=(
            jax.ShapeDtypeStruct((CHUNKS, SEGS, PART, ROWS), f32),
            jax.ShapeDtypeStruct((LEV, SEG, ROWS), f32),
            jax.ShapeDtypeStruct((LEV, 128, 256), f32),
        ),
        in_specs=[anywhere] * 7 + [vmem] * 3,
        out_specs=(anywhere,) * 3,
        scratch_shapes=[
            field, field, field, field,
            pltpu.VMEM((2 * RANK, WIDE), bf), pltpu.VMEM((4, 256, WIDE), bf), pltpu.VMEM((4, 2 * RANK, 768), bf),
            pltpu.VMEM((WIDE, 256), bf), pltpu.VMEM((WIDE, 256), bf),
            pltpu.VMEM((CHUNKS, 2, STEP, ROWS), f32), pltpu.VMEM((CHUNKS, 2, 2, STEP, ROWS), f32),
            pltpu.VMEM((CHUNKS, STEP, ROWS), f32), pltpu.VMEM((2, 2, LEV, 1, ROWS), f32),
            pltpu.VMEM((CHUNKS, SEGS, PART, ROWS), f32), pltpu.VMEM((CHUNKS, SEGS, PART, ROWS), f32),
            pltpu.VMEM((CHUNKS, SEGS, PART, ROWS), f32),
            pltpu.VMEM((16, 256), f32), pltpu.VMEM((SEGS, 16, 256), f32), pltpu.VMEM((2, LEV, SEGS, 256), f32),
            dma((CHUNKS, 4)), dma((3,)), dma((CHUNKS, 2)), dma((CHUNKS, 2)), dma((2, 2)), dma((2, 2)),
            dma((CHUNKS, SEGS)), dma((CHUNKS, SEGS)), dma((CHUNKS, SEGS)), dma((CHUNKS, SEGS)),
            dma((SEGS,)), dma((SEGS,)), dma((BANDS,)), dma((BANDS,)), dma((LEV + 1,)), dma((CHUNKS,)),
        ],
        compiler_params=pltpu.CompilerParams(
            collective_id=0, has_side_effects=True, vmem_limit_bytes=56 * 2**20
        ),
        cost_estimate=pl.CostEstimate(flops=10**9, bytes_accessed=16 * 10**6, transcendentals=0),
    )(
        flip(start), flip(sec), flip(zon), flip(mer), ut, pt, qt,
        cutoffs.reshape(BANDS, ROWS), rc, nest_values,
    )
    result = pl.pallas_call(
        finish_kernel,
        out_shape=jax.ShapeDtypeStruct((LEV, SEG, ROWS), f32),
        in_specs=[smem, vmem, vmem, anywhere, anywhere],
        out_specs=anywhere,
        scratch_shapes=[
            pltpu.VMEM((LEV, 256 + 928 + 256, ROWS), f32),
            pltpu.VMEM((LEV, 128, 256), f32),
            pltpu.VMEM((RANK, 2 * ROWS), f32),
            dma((LEV,)),
            dma,
        ],
        compiler_params=pltpu.CompilerParams(vmem_limit_bytes=56 * 2**20),
        cost_estimate=pl.CostEstimate(flops=10**9, bytes_accessed=4 * 10**6, transcendentals=0),
    )(nest_corners, zout, eu, sect, nestg)
    return flip(result)


def solution(mesh):
    tables = make_tables()
    spec = P(None, "lat", "lon")
    return jax.shard_map(
        lambda *args: shards(*args, tables),
        mesh=mesh,
        in_specs=(spec, spec, spec, spec, P(), P(None, None, ("lat", "lon"), None), P()),
        out_specs=spec,
        check_vma=False,
    )
```

```python
import functools
import math

import jax
import jax.numpy as jnp
import ml_dtypes
import numpy as np
from jax import lax
from jax.experimental import pallas as pl
from jax.experimental.pallas import tpu as pltpu
from jax.sharding import PartitionSpec as P

LEV, NLAT, NLON, KMAX = 6, 2048, 7200, 512
BANDS, SEGS = 16, 8
ROWS, SEG = NLAT // BANDS, NLON // SEGS
RANK = 160
PART = RANK // 4
CHUNKS, PAIR = 3, 2
STEP, STEPS = 32, 29
CELLS = STEP * STEPS
TALL = CELLS + 8
WIDE = 1024
MESH = pl.DeviceIdType.MESH
BF = ml_dtypes.bfloat16


def tri_solve(diag, off, shift, rhs):
    n, r = rhs.shape
    b = rhs.copy()
    d, u1, u2 = (np.zeros((n, r)) for _ in range(3))
    cd, cu, cb = diag[0] - shift, np.full(r, off[0]), b[0]
    for j in range(n - 1):
        nd, nu, sub = diag[j + 1] - shift, off[j + 1] if j + 2 < n else 0.0, off[j]
        swap = np.abs(sub) > np.abs(cd)
        p = np.where(swap, sub, np.where(cd == 0, 1e-30, cd))
        pu1, pu2, pb = np.where(swap, nd, cu), np.where(swap, nu, 0.0), np.where(swap, b[j + 1], cb)
        o, ou1 = np.where(swap, cd, sub), np.where(swap, cu, nd)
        ou2, ob = np.where(swap, 0.0, nu), np.where(swap, cb, b[j + 1])
        f = o / p
        d[j], u1[j], u2[j], b[j] = p, pu1, pu2, pb
        cd, cu, cb = ou1 - f * pu1, ou2 - f * pu2, ob - f * pb
    d[n - 1] = np.where(np.abs(cd) < 1e-20, 1e-20, cd)
    b[n - 1] = cb
    x = np.zeros((n, r))
    x[n - 1] = b[n - 1] / d[n - 1]
    x[n - 2] = (b[n - 2] - u1[n - 2] * x[n - 1]) / d[n - 2]
    for j in range(n - 3, -1, -1):
        x[j] = (b[j] - u1[j] * x[j + 1] - u2[j] * x[j + 2]) / d[j]
    return x


def slepian(length, width, rank):
    i = np.arange(length, dtype=np.float64)
    diag = ((length - 1 - 2 * i) / 2) ** 2 * np.cos(2 * np.pi * width)
    off = (i * (length - i) / 2)[1:]
    off2 = np.concatenate([[0.0], off**2])
    bound = np.abs(diag).max() + 2 * off.max()
    low, high, want = np.full(rank, -bound), np.full(rank, bound), np.arange(rank)
    for _ in range(70):
        mid = 0.5 * (low + high)
        above, q = np.zeros(rank, dtype=np.int64), np.ones(rank)
        for j in range(length):
            q = diag[j] - mid - off2[j] / q
            q = np.where(q == 0.0, 1e-300, q)
            above += q > 0
        up = above > want
        low, high = np.where(up, mid, low), np.where(up, high, mid)
    x = np.ones((length, rank)) + 0.3 * np.cos(i * i)[:, None]
    for _ in range(4):
        x = tri_solve(diag, off, 0.5 * (low + high), x)
        x = x / np.sqrt((x * x).sum(0))
    return x


def split(x):
    hi = x.astype(BF)
    return hi, (x - hi.astype(np.float64)).astype(BF)


def make_tables():
    basis = slepian(SEG, 512.0 / NLON, RANK)
    k, i = np.arange(KMAX), np.arange(SEG)
    waves = np.exp(-2j * np.pi * ((i[:, None] * k[None, :]) % NLON) / NLON)
    v = np.einsum("ir,ik->rk", basis, waves)
    weight = np.where(k == 0, 1.0, 2.0) / NLON
    uh, ul = split(basis)
    ut = np.zeros((2 * RANK, WIDE), BF)
    ut[:RANK, :SEG], ut[RANK:, :SEG] = uh.T, ul.T
    eu = np.zeros((CELLS, 512), BF)
    eu[:SEG, :RANK], eu[:SEG, RANK : 2 * RANK], eu[:SEG, 2 * RANK : 3 * RANK] = uh, uh, ul
    pt = np.zeros((4, 256, WIDE), BF)
    qt = np.zeros((4, 2 * RANK, 768), BF)
    for g in range(4):
        s1, s2 = g, (4 if g == 0 else 8 - g)
        k1, k2 = np.arange(64) * 8 + s1, np.arange(64) * 8 + s2
        v1, v2 = v[:, k1], v[:, k2]
        w1, w2 = weight[k1], weight[k2]
        z = np.zeros((RANK, 64))
        if g == 0:
            p = np.block([[v1.real, z, v1.imag, z], [z, v2.real, z, v2.imag]])
            q = np.block([[v1.real * w1, z, v1.imag * w1, z], [z, v2.real * w2, z, v2.imag * w2]])
        else:
            p = np.block([[v1.real, v2.real, v1.imag, v2.imag], [-v1.imag, v2.imag, v1.real, -v2.real]])
            q = np.block(
                [
                    [v1.real * w1, v2.real * w2, v1.imag * w1, v2.imag * w2],
                    [-v1.imag * w1, v2.imag * w2, v1.real * w1, -v2.real * w2],
                ]
            )
        ph, pl_ = split(p.T)
        pt[g, :, :320], pt[g, :, 320:640], pt[g, :, 640:960] = ph, ph, pl_
        qh, ql = split(q)
        qt[g, :, :256], qt[g, :, 256:512], qt[g, :, 512:] = qh, qh, ql
    step = np.float32(math.pi / NLAT)
    half = np.float32(math.pi / 2)
    e = np.arange(NLAT + 1)
    edge = np.cos((e.astype(np.float32) * step - half).astype(np.float64)).astype(np.float32)
    edge[0] = edge[-1] = 0.0
    center = np.cos(((np.arange(NLAT).astype(np.float32) + np.float32(0.5)) * step - half).astype(np.float64))
    rc = np.zeros((BANDS, 8, ROWS), np.float32)
    for b in range(BANDS):
        r0 = b * ROWS
        rc[b, 0, : ROWS - 1] = 0.0625 * edge[r0 + 1 : r0 + ROWS]
        rc[b, 1] = (1.0 / center[r0 : r0 + ROWS]).astype(np.float32)
        rc[b, 4, 0], rc[b, 4, ROWS - 1] = rc[b, 1, 0], -rc[b, 1, ROWS - 1]
        rc[b, 2] = 0.0625 * edge[r0]
        rc[b, 3] = 0.0625 * edge[r0 + ROWS]
    return ut, eu, pt, qt, rc


def lanes(shape):
    return lax.broadcasted_iota(jnp.int32, shape, len(shape) - 1)


def hi_lo(x):
    hi = x.astype(jnp.bfloat16)
    return hi, (x - hi.astype(jnp.float32)).astype(jnp.bfloat16)


def dot(a, b):
    return jnp.dot(a, b, preferred_element_type=jnp.float32)


def section_kernel(
    start, sec, zon, mer, ut_h, pt_h, qt_h, cut, rc, nest,
    zout, sect, nestg,
    sb, tb, zb, mb, ut, pt, qt, sh, sl, pk, pkr, lh,
    fsend, recv, bsend, nsend, ngat, nasm,
    ld, tabs, psend, precv, lsend, lrecv, fs, fr, bs, br, n1s, n1r, n2s, n2r, osem, zsem,
):
    lat, lon = lax.axis_index("lat"), lax.axis_index("lon")
    polar = (lat < BANDS // 4) | (lat >= BANDS - BANDS // 4)
    core = lax.rem(lon, 2)

    barrier = pltpu.get_barrier_semaphore()
    for k in range(1, SEGS):
        pl.semaphore_signal(barrier, inc=1, device_id=(lat, lax.rem(lon + k, SEGS)), device_id_type=MESH)
    for k in range(1, BANDS):
        pl.semaphore_signal(barrier, inc=1, device_id=(lax.rem(lat + k, BANDS), lon), device_id_type=MESH)

    loads = [[None] * 4 for _ in range(CHUNKS)]
    for late in range(2):
        for c in range(CHUNKS):
            pair = pl.ds(PAIR * c, PAIR)
            for a, (src, dst) in enumerate(((sec, tb), (mer, mb)) if late == 0 else ((zon, zb), (start, sb))):
                copy = pltpu.make_async_copy(src.at[pair], dst.at[pair, pl.ds(0, SEG)], ld.at[c, 2 * late + a])
                copy.start()
                loads[c][2 * late + a] = copy
    tables = [
        pltpu.make_async_copy(src, dst, tabs.at[n]) for n, (src, dst) in enumerate(((ut_h, ut), (pt_h, pt), (qt_h, qt)))
    ]
    for copy in tables:
        copy.start()

    for n in range(12):
        nsend[n : n + 1, :] = nest[n // 6, n % 6]
    nsend[12:16, :] = jnp.zeros((4, 256), jnp.float32)
    for buf in (tb, zb, mb, sb):
        for lev in range(LEV):
            buf[lev, SEG:TALL, :] = jnp.zeros((TALL - SEG, ROWS), jnp.float32)
    for c in range(CHUNKS):
        sh[c, CELLS:, :] = jnp.zeros((WIDE - CELLS, 256), jnp.bfloat16)
        sl[c, CELLS:, :] = jnp.zeros((WIDE - CELLS, 256), jnp.bfloat16)

    lane = lanes((STEP, ROWS))
    even = (lane & 1) == 0
    before, after = lax.rem(lat + BANDS - 1, BANDS), lax.rem(lat + 1, BANDS)
    left, right = lax.rem(lon + SEGS - 1, SEGS), lax.rem(lon + 1, SEGS)
    has_before, has_after = lat > 0, lat < BANDS - 1
    lat_copies, lon_copies, nest_copies = [], [], []
    for c in range(CHUNKS):
        loads[c][0].wait()
        loads[c][1].wait()

        def pack(b, acc, c=c):
            out = []
            for buf, x in zip((tb, mb), acc):
                for h in range(PAIR):
                    v = buf[PAIR * c + h, pl.ds(pl.multiple_of(b * STEP, STEP), STEP), :]
                    x = jnp.where((lane >> 1) == 2 * b + h, pltpu.roll(v, lax.rem(4 * b + 2 * h + 1, ROWS), 1), x)
                out.append(x)
            return tuple(out)

        none = jnp.zeros((STEP, ROWS), jnp.float32)
        packed = lax.fori_loop(0, STEPS, pack, (none, none), unroll=True)
        for a in range(2):
            pk[c, a] = packed[a]
        if c == 0:
            pl.semaphore_wait(barrier, SEGS - 1 + BANDS - 1)
        for way, (to, there_is) in enumerate(((after, has_after), (before, has_before))):
            copy = pltpu.make_async_remote_copy(
                src_ref=pk.at[c], dst_ref=pkr.at[c, way], send_sem=psend.at[c, way], recv_sem=precv.at[c, way],
                device_id=(to, lon), device_id_type=MESH,
            )
            pl.when(there_is)(copy.start)
            lat_copies.append(copy)
        if c == 0:
            for a, src in enumerate((sec, zon)):
                for way, (row, to) in enumerate(((0, left), (SEG - 1, right))):
                    copy = pltpu.make_async_remote_copy(
                        src_ref=src.at[:, pl.ds(row, 1), :], dst_ref=lh.at[a, way], send_sem=lsend.at[a, way],
                        recv_sem=lrecv.at[a, way], device_id=(lat, to), device_id_type=MESH,
                    )
                    copy.start()
                    lon_copies.append(copy)

    for way, there_is in enumerate((has_before, has_after)):

        @pl.when(jnp.logical_not(there_is))
        def _(way=way):
            for c in range(CHUNKS):
                for a in range(2):
                    pkr[c, way, a] = jnp.zeros((STEP, ROWS), jnp.float32)

    for k in range(1, SEGS):
        copy = pltpu.make_async_remote_copy(
            src_ref=nsend, dst_ref=ngat.at[lon], send_sem=n1s.at[k], recv_sem=n1r.at[k],
            device_id=(lat, lax.rem(lon + k, SEGS)), device_id_type=MESH,
        )
        copy.start()
        nest_copies.append(copy)
    ngat[lon] = nsend[...]

    edge_row = rc[lat, 0:1, :]
    inverse_cos = rc[lat, 1:2, :]
    first_edge, last_edge = rc[lat, 2:3, :], rc[lat, 3:4, :]
    end_scale = rc[lat, 4:5, :]
    flux_scale = jnp.where(even[:1], last_edge, first_edge)

    def inner(c):
        for copy in loads[c][2:]:
            copy.wait()
        for lev in range(PAIR * c, PAIR * c + PAIR):
            t_all, z_all = tb[lev], zb[lev]
            t = t_all[:CELLS]
            east = 0.0625 * (z_all[:CELLS] + z_all[1 : CELLS + 1]) * (t + t_all[1 : CELLS + 1])
            zonal = east - jnp.concatenate([jnp.zeros((1, ROWS), jnp.float32), east[: CELLS - 1]], axis=0)
            m = mb[lev, :CELLS, :]
            south = edge_row * (t + pltpu.roll(t, ROWS - 1, 1)) * (m + pltpu.roll(m, ROWS - 1, 1))
            north = pltpu.roll(south, 1, 1)
            sb[lev, :CELLS, :] = 0.75 * sb[lev, :CELLS, :] + 0.25 * t - zonal - inverse_cos * (south - north)

    for c in range(CHUNKS):
        inner(c)

    eight = pl.ds(pl.multiple_of(lat * SEGS, SEGS), SEGS)
    mine, other = pl.ds(LEV // 2 * core, LEV // 2), pl.ds(LEV // 2 * (1 - core), LEV // 2)
    spread = []
    for k in range(1, BANDS):
        to = lax.rem(lat + k, BANDS)
        copy = pltpu.make_async_remote_copy(
            src_ref=nasm.at[to // (BANDS // 2), mine], dst_ref=nestg.at[mine, eight, :], send_sem=n2s.at[k],
            recv_sem=n2r.at[k], device_id=(to, lon), device_id_type=MESH,
        )
        spread.append(copy)
    own_nest = pltpu.make_async_copy(nasm.at[lat // (BANDS // 2), mine], nestg.at[mine, eight, :], osem.at[LEV])
    swap = pltpu.make_async_remote_copy(
        src_ref=nestg.at[mine], dst_ref=nestg.at[mine], send_sem=n2s.at[0], recv_sem=n2r.at[0],
        device_id=(lat, lon + 1 - 2 * core), device_id_type=MESH,
    )

    def spread_nest():
        for copy in nest_copies:
            copy.wait_recv()
        for n in range(12):
            nasm[n // 6, n % 6] = jnp.concatenate([ngat[d, n : n + 1, :] for d in range(SEGS)], axis=0)
        for copy in spread:
            copy.start()
        own_nest.start()

    def swap_nest():
        for copy in spread:
            copy.wait_recv()
        own_nest.wait()
        swap.start()

    for copy in lon_copies:
        copy.wait_recv()

    def borders(c, put):
        for way, there_is in enumerate((has_before, has_after)):
            pl.when(there_is)(lat_copies[2 * c + way].wait_recv)
        sums = [
            pk[c, a] + jnp.where(even, pltpu.roll(pkr[c, 1, a], ROWS - 1, 1), pltpu.roll(pkr[c, 0, a], 1, 1))
            for a in range(2)
        ]
        packed = sums[0] * sums[1] * flux_scale
        for h in range(PAIR):
            lev = PAIR * c + h
            t0, z0 = tb[lev, 0:1, :], zb[lev, 0:1, :]
            t1, z1 = tb[lev, SEG - 1 : SEG, :], zb[lev, SEG - 1 : SEG, :]
            west = 0.0625 * (lh[1, 1, lev] + z0) * (lh[0, 1, lev] + t0)
            east = 0.0625 * (lh[1, 0, lev] + z1) * (lh[0, 0, lev] + t1)
            sb[lev, 0:1, :] = sb[lev, 0:1, :] + west
            sb[lev, SEG - 1 : SEG, :] = sb[lev, SEG - 1 : SEG, :] - (east - 0.0625 * z1 * t1)
            ends = jnp.concatenate(
                [pltpu.roll(packed, (2 * ROWS - 1 - 4 * b - 2 * h) % ROWS, 1) for b in range(STEPS)], axis=0
            )
            put(lev, h, sb[lev, :CELLS, :] + end_scale * ends)

    @pl.when(jnp.logical_not(polar))
    def _():
        def put(lev, h, value):
            sb[lev, :CELLS, :] = value

        outs = []
        for c in range(CHUNKS):
            borders(c, put)
            if c == 0:
                spread_nest()
            pair = pl.ds(PAIR * c, PAIR)
            copy = pltpu.make_async_copy(sb.at[pair, pl.ds(0, SEG)], sect.at[pair], osem.at[c])
            copy.start()
            outs.append(copy)
        swap_nest()
        for copy in outs:
            copy.wait()
        for copy in tables:
            copy.wait()

    @pl.when(polar)
    def _():
        def put(c, lev, h, value):
            hi, lo = hi_lo(value)
            sh[c, :CELLS, h * ROWS : (h + 1) * ROWS] = hi
            sl[c, :CELLS, h * ROWS : (h + 1) * ROWS] = lo

        block = lanes((PART, ROWS)) // 32

        def exchange(c, k, src, dst, send, receive):
            return pltpu.make_async_remote_copy(
                src_ref=src.at[c, lax.rem(lon + k, SEGS)], dst_ref=dst.at[c, lon], send_sem=send.at[c, k],
                recv_sem=receive.at[c, k], device_id=(lat, lax.rem(lon + k, SEGS)), device_id_type=MESH,
            )

        there = []
        for c in range(CHUNKS):
            borders(c, functools.partial(put, c))
            if c == 0:
                tables[0].wait()
            both = dot(ut[...], sh[c])
            y = both[:RANK] + both[RANK:] + dot(ut[:RANK, :], sl[c])
            for h in range(PAIR):
                for q in range(4):
                    acc = None
                    for j in range(4):
                        v = y[PART * j : PART * (j + 1), ROWS * h : ROWS * (h + 1)]
                        if j != q:
                            v = pltpu.roll(v, (32 * (j - q)) % ROWS, 1)
                        acc = v if acc is None else jnp.where(block == j, v, acc)
                    fsend[c, 4 * h + q] = acc
            recv[c, lon] = fsend[c, lon]
            there.append([exchange(c, k, fsend, recv, fs, fr) for k in range(1, SEGS)])
            for copy in there[c]:
                copy.start()
            if c == 0:
                spread_nest()

        tables[1].wait()
        tables[2].wait()
        rows_cut = pltpu.roll(jnp.broadcast_to(cut[pl.ds(lat, 1), :], (8, ROWS)), ROWS - 32 * lax.rem(lon, 4), 1)[:1]
        n = lax.broadcasted_iota(jnp.int32, (256, ROWS), 0)
        root = math.sqrt(0.5)
        back, own = [], []
        for c in range(CHUNKS):
            for copy in there[c]:
                copy.wait_recv()
            y = [recv[c, d] for d in range(SEGS)]
            u = [y[j] + y[j + 4] for j in range(4)]
            v = [y[j] - y[j + 4] for j in range(4)]
            a, b, m, p = u[0] + u[2], u[1] + u[3], root * (v[1] - v[3]), root * (v[1] + v[3])
            groups = [(a + b, a - b), (v[0] + m, -v[2] - p), (u[0] - u[2], u[3] - u[1]), (v[0] - m, v[2] - p)]
            spectra = []
            for g, two in enumerate(groups):
                tall = jnp.concatenate(
                    [x if j == 0 else pltpu.roll(x, ROWS - 32 * j, 1) for x in two for j in range(4)], axis=0
                )
                hi, lo = hi_lo(tall)
                rhs = jnp.concatenate([hi, lo, hi, jnp.zeros((WIDE - 960, ROWS), jnp.bfloat16)], axis=0)
                wave = dot(pt[g], rhs)
                number = 8 * (n & 63) + jnp.where((n & 64) == 0, g, 4 if g == 0 else 8 - g)
                wave = jnp.where(number <= rows_cut, wave, 0.0)
                hi, lo = hi_lo(wave)
                full = dot(qt[g], jnp.concatenate([hi, lo, hi], axis=0))
                for x in range(2):
                    acc = None
                    for j in range(4):
                        w = full[RANK * x + PART * j : RANK * x + PART * (j + 1)]
                        if j:
                            w = pltpu.roll(w, 32 * j, 1)
                        acc = w if acc is None else jnp.where(block == j, w, acc)
                    spectra.append(acc)
            w0, w4, r1, i1, r2, i2, r3, i3 = spectra
            plus, minus = w0 + w4, w0 - w4
            evens = [plus + r2, minus - i2, plus - r2, minus + i2]
            d1, d2 = root * (r1 - r3), root * (i1 + i3)
            odds = [r1 + r3, d1 - d2, i3 - i1, -d1 - d2]
            for e in range(4):
                bsend[c, e] = evens[e] + odds[e]
                bsend[c, e + 4] = evens[e] - odds[e]
            back.append([exchange(c, k, bsend, zout, bs, br) for k in range(1, SEGS)])
            for copy in back[c]:
                copy.start()
            copy = pltpu.make_async_copy(bsend.at[c, lon], zout.at[c, lon], zsem.at[c])
            copy.start()
            own.append(copy)
        swap_nest()
        for c in range(CHUNKS):
            own[c].wait()
            for copy in back[c]:
                copy.wait_recv()
        for c in range(CHUNKS):
            for copy in there[c] + back[c]:
                copy.wait_send()

    swap.wait()
    for copy in lon_copies + nest_copies + spread:
        copy.wait_send()
    for n, copy in enumerate(lat_copies):
        pl.when((has_after, has_before)[n % 2])(copy.wait_send)


def finish_kernel(corners, zin, eu, sect, nestg, out, ob, nb, zc, osem, ssem, nsem):
    lat, lon = lax.axis_index("lat"), lax.axis_index("lon")
    polar = (lat < BANDS // 4) | (lat >= BANDS - BANDS // 4)
    half = lat // (BANDS // 2)
    row = corners[half, 0] - lat * ROWS
    col = corners[half, 1] - lon * SEG
    hit = (row > -ROWS) & (row < ROWS) & (col > -256) & (col < SEG)
    miss = jnp.logical_not(hit)
    fetch = pltpu.make_async_copy(nestg, nb, nsem)
    copies = [
        pltpu.make_async_copy(
            ob.at[pl.ds(PAIR * c, PAIR), pl.ds(256, SEG), :], out.at[pl.ds(PAIR * c, PAIR)], osem.at[c]
        )
        for c in range(CHUNKS)
    ]
    fills = [
        pltpu.make_async_copy(
            sect.at[pl.ds(PAIR * c, PAIR)], ob.at[pl.ds(PAIR * c, PAIR), pl.ds(256, SEG), :], ssem.at[c]
        )
        for c in range(CHUNKS)
    ]
    block = lanes((PART, ROWS)) // 32

    @pl.when(jnp.logical_not(polar))
    def _():
        for copy in fills:
            copy.start()

    @pl.when(hit)
    def _():
        fetch.start()

    @pl.when(jnp.logical_not(polar))
    def _():
        for c in range(CHUNKS):
            fills[c].wait()

            @pl.when(miss)
            def _():
                copies[c].start()

    @pl.when(polar)
    def _():
        for c in range(CHUNKS):
            for h in range(PAIR):
                for j in range(4):
                    acc = None
                    for q in range(4):
                        v = zin[c, 4 * h + q]
                        if j != q:
                            v = pltpu.roll(v, (32 * (q - j)) % ROWS, 1)
                        acc = v if acc is None else jnp.where(block == q, v, acc)
                    zc[PART * j : PART * (j + 1), h * ROWS : (h + 1) * ROWS] = acc
            hi, lo = hi_lo(zc[...])
            rhs = jnp.concatenate([hi, lo, hi, jnp.zeros((32, 2 * ROWS), jnp.bfloat16)], axis=0)
            full = dot(eu[...], rhs)
            for h in range(PAIR):
                ob[PAIR * c + h, 256 : 256 + CELLS, :] = full[:, h * ROWS : (h + 1) * ROWS]

            @pl.when(miss)
            def _():
                copies[c].start()

    @pl.when(hit)
    def _():
        fetch.wait()
        lane = lanes((264, ROWS))
        cell = lax.broadcasted_iota(jnp.int32, (264, ROWS), 0)
        place = col + 256
        base = pl.multiple_of((place // 8) * 8, 8)
        off = place - base
        inside = (lane >= row) & (lane < row + ROWS) & (cell >= off) & (cell < off + 256)
        for lev in range(LEV):
            flat = jnp.swapaxes(nb[lev], 0, 1)
            tall = jnp.concatenate([flat, jnp.zeros((8, ROWS), jnp.float32)], axis=0)
            tall = pltpu.roll(pltpu.roll(tall, off, 0), lax.rem(row + ROWS, ROWS), 1)
            here = ob[lev, pl.ds(base, 264), :]
            ob[lev, pl.ds(base, 264), :] = jnp.where(inside, tall, here)
            if lev % PAIR == PAIR - 1:
                copies[lev // PAIR].start()

    for copy in copies:
        copy.wait()


def shards(start, sec, zon, mer, cutoffs, nest_values, nest_corners, tables):
    ut, eu, pt, qt, rc = (jnp.asarray(x) for x in tables)
    flip = lambda x: jnp.swapaxes(x, 1, 2)
    anywhere = pl.BlockSpec(memory_space=pl.ANY)
    vmem = pl.BlockSpec(memory_space=pltpu.VMEM)
    smem = pl.BlockSpec(memory_space=pltpu.SMEM)
    f32, bf = jnp.float32, jnp.bfloat16
    dma = pltpu.SemaphoreType.DMA
    field = pltpu.VMEM((LEV, TALL, ROWS), f32)
    zout, sect, nestg = pl.pallas_call(
        section_kernel,
        out_shape=(
            jax.ShapeDtypeStruct((CHUNKS, SEGS, PART, ROWS), f32),
            jax.ShapeDtypeStruct((LEV, SEG, ROWS), f32),
            jax.ShapeDtypeStruct((LEV, 128, 256), f32),
        ),
        in_specs=[anywhere] * 7 + [vmem] * 3,
        out_specs=(anywhere,) * 3,
        scratch_shapes=[
            field, field, field, field,
            pltpu.VMEM((2 * RANK, WIDE), bf), pltpu.VMEM((4, 256, WIDE), bf), pltpu.VMEM((4, 2 * RANK, 768), bf),
            pltpu.VMEM((CHUNKS, WIDE, 256), bf), pltpu.VMEM((CHUNKS, WIDE, 256), bf),
            pltpu.VMEM((CHUNKS, 2, STEP, ROWS), f32), pltpu.VMEM((CHUNKS, 2, 2, STEP, ROWS), f32),
            pltpu.VMEM((2, 2, LEV, 1, ROWS), f32),
            pltpu.VMEM((CHUNKS, SEGS, PART, ROWS), f32), pltpu.VMEM((CHUNKS, SEGS, PART, ROWS), f32),
            pltpu.VMEM((CHUNKS, SEGS, PART, ROWS), f32),
            pltpu.VMEM((16, 256), f32), pltpu.VMEM((SEGS, 16, 256), f32), pltpu.VMEM((2, LEV, SEGS, 256), f32),
            dma((CHUNKS, 4)), dma((3,)), dma((CHUNKS, 2)), dma((CHUNKS, 2)), dma((2, 2)), dma((2, 2)),
            dma((CHUNKS, SEGS)), dma((CHUNKS, SEGS)), dma((CHUNKS, SEGS)), dma((CHUNKS, SEGS)),
            dma((SEGS,)), dma((SEGS,)), dma((BANDS,)), dma((BANDS,)), dma((LEV + 1,)), dma((CHUNKS,)),
        ],
        compiler_params=pltpu.CompilerParams(
            collective_id=0, has_side_effects=True, vmem_limit_bytes=56 * 2**20
        ),
        cost_estimate=pl.CostEstimate(flops=10**9, bytes_accessed=16 * 10**6, transcendentals=0),
    )(
        flip(start), flip(sec), flip(zon), flip(mer), ut, pt, qt,
        cutoffs.reshape(BANDS, ROWS), rc, nest_values,
    )
    result = pl.pallas_call(
        finish_kernel,
        out_shape=jax.ShapeDtypeStruct((LEV, SEG, ROWS), f32),
        in_specs=[smem, vmem, vmem, anywhere, anywhere],
        out_specs=anywhere,
        scratch_shapes=[
            pltpu.VMEM((LEV, 256 + 928 + 256, ROWS), f32),
            pltpu.VMEM((LEV, 128, 256), f32),
            pltpu.VMEM((RANK, 2 * ROWS), f32),
            dma((CHUNKS,)),
            dma((CHUNKS,)),
            dma,
        ],
        compiler_params=pltpu.CompilerParams(vmem_limit_bytes=56 * 2**20),
        cost_estimate=pl.CostEstimate(flops=10**9, bytes_accessed=4 * 10**6, transcendentals=0),
    )(nest_corners, zout, eu, sect, nestg)
    return flip(result)


def solution(mesh):
    tables = make_tables()
    spec = P(None, "lat", "lon")
    return jax.shard_map(
        lambda *args: shards(*args, tables),
        mesh=mesh,
        in_specs=(spec, spec, spec, spec, P(), P(None, None, ("lat", "lon"), None), P()),
        out_specs=spec,
        check_vma=False,
    )
```

```python
import functools
import math

import jax
import jax.numpy as jnp
import ml_dtypes
import numpy as np
from jax import lax
from jax.experimental import pallas as pl
from jax.experimental.pallas import tpu as pltpu
from jax.sharding import PartitionSpec as P

LEV, NLAT, NLON, KMAX = 6, 2048, 7200, 512
BANDS, SEGS = 16, 8
ROWS, SEG = NLAT // BANDS, NLON // SEGS
RANK = 160
PART = RANK // 4
CHUNKS, PAIR = 3, 2
STEP, STEPS = 32, 29
CELLS = STEP * STEPS
TALL = CELLS + 8
WIDE = 1024
MESH = pl.DeviceIdType.MESH
BF = ml_dtypes.bfloat16


def tri_solve(diag, off, shift, rhs):
    n, r = rhs.shape
    b = rhs.copy()
    d, u1, u2 = (np.zeros((n, r)) for _ in range(3))
    cd, cu, cb = diag[0] - shift, np.full(r, off[0]), b[0]
    for j in range(n - 1):
        nd, nu, sub = diag[j + 1] - shift, off[j + 1] if j + 2 < n else 0.0, off[j]
        swap = np.abs(sub) > np.abs(cd)
        p = np.where(swap, sub, np.where(cd == 0, 1e-30, cd))
        pu1, pu2, pb = np.where(swap, nd, cu), np.where(swap, nu, 0.0), np.where(swap, b[j + 1], cb)
        o, ou1 = np.where(swap, cd, sub), np.where(swap, cu, nd)
        ou2, ob = np.where(swap, 0.0, nu), np.where(swap, cb, b[j + 1])
        f = o / p
        d[j], u1[j], u2[j], b[j] = p, pu1, pu2, pb
        cd, cu, cb = ou1 - f * pu1, ou2 - f * pu2, ob - f * pb
    d[n - 1] = np.where(np.abs(cd) < 1e-20, 1e-20, cd)
    b[n - 1] = cb
    x = np.zeros((n, r))
    x[n - 1] = b[n - 1] / d[n - 1]
    x[n - 2] = (b[n - 2] - u1[n - 2] * x[n - 1]) / d[n - 2]
    for j in range(n - 3, -1, -1):
        x[j] = (b[j] - u1[j] * x[j + 1] - u2[j] * x[j + 2]) / d[j]
    return x


def slepian(length, width, rank):
    i = np.arange(length, dtype=np.float64)
    diag = ((length - 1 - 2 * i) / 2) ** 2 * np.cos(2 * np.pi * width)
    off = (i * (length - i) / 2)[1:]
    off2 = np.concatenate([[0.0], off**2])
    bound = np.abs(diag).max() + 2 * off.max()
    low, high, want = np.full(rank, -bound), np.full(rank, bound), np.arange(rank)
    for _ in range(70):
        mid = 0.5 * (low + high)
        above, q = np.zeros(rank, dtype=np.int64), np.ones(rank)
        for j in range(length):
            q = diag[j] - mid - off2[j] / q
            q = np.where(q == 0.0, 1e-300, q)
            above += q > 0
        up = above > want
        low, high = np.where(up, mid, low), np.where(up, high, mid)
    x = np.ones((length, rank)) + 0.3 * np.cos(i * i)[:, None]
    for _ in range(4):
        x = tri_solve(diag, off, 0.5 * (low + high), x)
        x = x / np.sqrt((x * x).sum(0))
    return x


def split(x):
    hi = x.astype(BF)
    return hi, (x - hi.astype(np.float64)).astype(BF)


def make_tables():
    basis = slepian(SEG, 512.0 / NLON, RANK)
    k, i = np.arange(KMAX), np.arange(SEG)
    waves = np.exp(-2j * np.pi * ((i[:, None] * k[None, :]) % NLON) / NLON)
    v = np.einsum("ir,ik->rk", basis, waves)
    weight = np.where(k == 0, 1.0, 2.0) / NLON
    uh, ul = split(basis)
    ut = np.zeros((2 * RANK, WIDE), BF)
    ut[:RANK, :SEG], ut[RANK:, :SEG] = uh.T, ul.T
    eu = np.zeros((CELLS, 512), BF)
    eu[:SEG, :RANK], eu[:SEG, RANK : 2 * RANK], eu[:SEG, 2 * RANK : 3 * RANK] = uh, uh, ul
    pt = np.zeros((4, 256, 4 * RANK), BF)
    qt = np.zeros((4, 2 * RANK, 512), BF)
    for g in range(4):
        s1, s2 = g, (4 if g == 0 else 8 - g)
        k1, k2 = np.arange(64) * 8 + s1, np.arange(64) * 8 + s2
        v1, v2 = v[:, k1], v[:, k2]
        w1, w2 = weight[k1], weight[k2]
        z = np.zeros((RANK, 64))
        if g == 0:
            p = np.block([[v1.real, z, v1.imag, z], [z, v2.real, z, v2.imag]])
            q = np.block([[v1.real * w1, z, v1.imag * w1, z], [z, v2.real * w2, z, v2.imag * w2]])
        else:
            p = np.block([[v1.real, v2.real, v1.imag, v2.imag], [-v1.imag, v2.imag, v1.real, -v2.real]])
            q = np.block(
                [
                    [v1.real * w1, v2.real * w2, v1.imag * w1, v2.imag * w2],
                    [-v1.imag * w1, v2.imag * w2, v1.real * w1, -v2.real * w2],
                ]
            )
        ph, pl_ = split(p.T)
        pt[g, :, : 2 * RANK], pt[g, :, 2 * RANK :] = ph, pl_
        qh, ql = split(q)
        qt[g, :, :256], qt[g, :, 256:] = qh, ql
    step = np.float32(math.pi / NLAT)
    half = np.float32(math.pi / 2)
    e = np.arange(NLAT + 1)
    edge = np.cos((e.astype(np.float32) * step - half).astype(np.float64)).astype(np.float32)
    edge[0] = edge[-1] = 0.0
    center = np.cos(((np.arange(NLAT).astype(np.float32) + np.float32(0.5)) * step - half).astype(np.float64))
    rc = np.zeros((BANDS, 8, ROWS), np.float32)
    for b in range(BANDS):
        r0 = b * ROWS
        rc[b, 0, : ROWS - 1] = 0.0625 * edge[r0 + 1 : r0 + ROWS]
        rc[b, 1] = (1.0 / center[r0 : r0 + ROWS]).astype(np.float32)
        rc[b, 4, 0], rc[b, 4, ROWS - 1] = rc[b, 1, 0], -rc[b, 1, ROWS - 1]
        rc[b, 2] = 0.0625 * edge[r0]
        rc[b, 3] = 0.0625 * edge[r0 + ROWS]
    return ut, eu, pt, qt, rc


def lanes(shape):
    return lax.broadcasted_iota(jnp.int32, shape, len(shape) - 1)


def hi_lo(x):
    hi = x.astype(jnp.bfloat16)
    return hi, (x - hi.astype(jnp.float32)).astype(jnp.bfloat16)


def dot(a, b):
    return jnp.dot(a, b, preferred_element_type=jnp.float32)


def split_dot(table, x):
    hi, lo = hi_lo(x)
    rhs = jnp.concatenate(
        [jnp.concatenate([hi, lo], axis=1), jnp.concatenate([hi, jnp.zeros_like(lo)], axis=1)], axis=0
    )
    both = dot(table, rhs)
    return both[:, : x.shape[1]] + both[:, x.shape[1] :]


def section_kernel(
    start, sec, zon, mer, ut_h, pt_h, qt_h, cut, rc, nest,
    zout, sect, nestg,
    sb, tb, zb, mb, ut, pt, qt, sh, sl, pk, pkr, lh,
    fsend, recv, bsend, nsend, ngat, nasm,
    ld, tabs, psend, precv, lsend, lrecv, fs, fr, bs, br, n1s, n1r, n2s, n2r, osem, zsem,
):
    lat, lon = lax.axis_index("lat"), lax.axis_index("lon")
    polar = (lat < BANDS // 4) | (lat >= BANDS - BANDS // 4)
    core = lax.rem(lon, 2)

    barrier = pltpu.get_barrier_semaphore()
    for k in range(1, SEGS):
        pl.semaphore_signal(barrier, inc=1, device_id=(lat, lax.rem(lon + k, SEGS)), device_id_type=MESH)
    for k in range(1, BANDS):
        pl.semaphore_signal(barrier, inc=1, device_id=(lax.rem(lat + k, BANDS), lon), device_id_type=MESH)

    loads = [
        [
            pltpu.make_async_copy(
                src.at[pl.ds(PAIR * c, PAIR)], dst.at[pl.ds(PAIR * c, PAIR), pl.ds(0, SEG)], ld.at[c, a]
            )
            for a, (src, dst) in enumerate(((sec, tb), (mer, mb), (zon, zb), (start, sb)))
        ]
        for c in range(CHUNKS)
    ]
    tables = [
        pltpu.make_async_copy(src, dst, tabs.at[n]) for n, (src, dst) in enumerate(((ut_h, ut), (pt_h, pt), (qt_h, qt)))
    ]
    for copy in loads[0] + tables[:1] + loads[1] + loads[2] + tables[1:]:
        copy.start()

    for n in range(12):
        nsend[n : n + 1, :] = nest[n // 6, n % 6]
    nsend[12:16, :] = jnp.zeros((4, 256), jnp.float32)
    for buf in (tb, zb, mb, sb):
        for lev in range(LEV):
            buf[lev, SEG:TALL, :] = jnp.zeros((TALL - SEG, ROWS), jnp.float32)
    for c in range(CHUNKS):
        sh[c, CELLS:, :] = jnp.zeros((WIDE - CELLS, 256), jnp.bfloat16)
        sl[c, CELLS:, :] = jnp.zeros((WIDE - CELLS, 256), jnp.bfloat16)

    lane = lanes((STEP, ROWS))
    even = (lane & 1) == 0
    before, after = lax.rem(lat + BANDS - 1, BANDS), lax.rem(lat + 1, BANDS)
    left, right = lax.rem(lon + SEGS - 1, SEGS), lax.rem(lon + 1, SEGS)
    has_before, has_after = lat > 0, lat < BANDS - 1
    lat_copies, lon_copies, nest_copies = [], [], []
    def send_halo(c):
        loads[c][0].wait()
        loads[c][1].wait()

        def pack(b, acc, c=c):
            out = []
            for buf, x in zip((tb, mb), acc):
                for h in range(PAIR):
                    v = buf[PAIR * c + h, pl.ds(pl.multiple_of(b * STEP, STEP), STEP), :]
                    x = jnp.where((lane >> 1) == 2 * b + h, pltpu.roll(v, lax.rem(4 * b + 2 * h + 1, ROWS), 1), x)
                out.append(x)
            return tuple(out)

        none = jnp.zeros((STEP, ROWS), jnp.float32)
        packed = lax.fori_loop(0, STEPS, pack, (none, none), unroll=True)
        for a in range(2):
            pk[c, a] = packed[a]
        if c == 0:
            pl.semaphore_wait(barrier, SEGS - 1 + BANDS - 1)
        for way, (to, there_is) in enumerate(((after, has_after), (before, has_before))):
            copy = pltpu.make_async_remote_copy(
                src_ref=pk.at[c], dst_ref=pkr.at[c, way], send_sem=psend.at[c, way], recv_sem=precv.at[c, way],
                device_id=(to, lon), device_id_type=MESH,
            )
            pl.when(there_is)(copy.start)
            lat_copies.append(copy)
        if c == 0:
            for a, src in enumerate((sec, zon)):
                for way, (row, to) in enumerate(((0, left), (SEG - 1, right))):
                    copy = pltpu.make_async_remote_copy(
                        src_ref=src.at[:, pl.ds(row, 1), :], dst_ref=lh.at[a, way], send_sem=lsend.at[a, way],
                        recv_sem=lrecv.at[a, way], device_id=(lat, to), device_id_type=MESH,
                    )
                    copy.start()
                    lon_copies.append(copy)

    send_halo(0)
    for way, there_is in enumerate((has_before, has_after)):

        @pl.when(jnp.logical_not(there_is))
        def _(way=way):
            for c in range(CHUNKS):
                for a in range(2):
                    pkr[c, way, a] = jnp.zeros((STEP, ROWS), jnp.float32)

    for k in range(1, SEGS):
        copy = pltpu.make_async_remote_copy(
            src_ref=nsend, dst_ref=ngat.at[lon], send_sem=n1s.at[k], recv_sem=n1r.at[k],
            device_id=(lat, lax.rem(lon + k, SEGS)), device_id_type=MESH,
        )
        copy.start()
        nest_copies.append(copy)
    ngat[lon] = nsend[...]

    edge_row = rc[lat, 0:1, :]
    inverse_cos = rc[lat, 1:2, :]
    first_edge, last_edge = rc[lat, 2:3, :], rc[lat, 3:4, :]
    end_scale = rc[lat, 4:5, :]
    flux_scale = jnp.where(even[:1], last_edge, first_edge)

    def inner(c):
        for copy in loads[c][2:]:
            copy.wait()
        for lev in range(PAIR * c, PAIR * c + PAIR):
            t_all, z_all = tb[lev], zb[lev]
            t = t_all[:CELLS]
            east = 0.0625 * (z_all[:CELLS] + z_all[1 : CELLS + 1]) * (t + t_all[1 : CELLS + 1])
            zonal = east - jnp.concatenate([jnp.zeros((1, ROWS), jnp.float32), east[: CELLS - 1]], axis=0)
            m = mb[lev, :CELLS, :]
            south = edge_row * (t + pltpu.roll(t, ROWS - 1, 1)) * (m + pltpu.roll(m, ROWS - 1, 1))
            north = pltpu.roll(south, 1, 1)
            sb[lev, :CELLS, :] = 0.75 * sb[lev, :CELLS, :] + 0.25 * t - zonal - inverse_cos * (south - north)

    inner(0)
    for c in range(1, CHUNKS):
        send_halo(c)

    eight = pl.ds(pl.multiple_of(lat * SEGS, SEGS), SEGS)
    mine, other = pl.ds(LEV // 2 * core, LEV // 2), pl.ds(LEV // 2 * (1 - core), LEV // 2)
    spread = []
    for k in range(1, BANDS):
        to = lax.rem(lat + k, BANDS)
        copy = pltpu.make_async_remote_copy(
            src_ref=nasm.at[to // (BANDS // 2), mine], dst_ref=nestg.at[mine, eight, :], send_sem=n2s.at[k],
            recv_sem=n2r.at[k], device_id=(to, lon), device_id_type=MESH,
        )
        spread.append(copy)
    own_nest = pltpu.make_async_copy(nasm.at[lat // (BANDS // 2), mine], nestg.at[mine, eight, :], osem.at[LEV])
    swap = pltpu.make_async_remote_copy(
        src_ref=nestg.at[mine], dst_ref=nestg.at[mine], send_sem=n2s.at[0], recv_sem=n2r.at[0],
        device_id=(lat, lon + 1 - 2 * core), device_id_type=MESH,
    )

    def spread_nest():
        for copy in nest_copies:
            copy.wait_recv()
        for n in range(12):
            nasm[n // 6, n % 6] = jnp.concatenate([ngat[d, n : n + 1, :] for d in range(SEGS)], axis=0)
        for copy in spread:
            copy.start()
        own_nest.start()

    def swap_nest():
        for copy in spread:
            copy.wait_recv()
        own_nest.wait()
        swap.start()

    def borders(c, put):
        if c == 0:
            for copy in lon_copies:
                copy.wait_recv()
        for way, there_is in enumerate((has_before, has_after)):
            pl.when(there_is)(lat_copies[2 * c + way].wait_recv)
        sums = [
            pk[c, a] + jnp.where(even, pltpu.roll(pkr[c, 1, a], ROWS - 1, 1), pltpu.roll(pkr[c, 0, a], 1, 1))
            for a in range(2)
        ]
        packed = sums[0] * sums[1] * flux_scale
        for h in range(PAIR):
            lev = PAIR * c + h
            t0, z0 = tb[lev, 0:1, :], zb[lev, 0:1, :]
            t1, z1 = tb[lev, SEG - 1 : SEG, :], zb[lev, SEG - 1 : SEG, :]
            west = 0.0625 * (lh[1, 1, lev] + z0) * (lh[0, 1, lev] + t0)
            east = 0.0625 * (lh[1, 0, lev] + z1) * (lh[0, 0, lev] + t1)
            sb[lev, 0:1, :] = sb[lev, 0:1, :] + west
            sb[lev, SEG - 1 : SEG, :] = sb[lev, SEG - 1 : SEG, :] - (east - 0.0625 * z1 * t1)
            ends = jnp.concatenate(
                [pltpu.roll(packed, (2 * ROWS - 1 - 4 * b - 2 * h) % ROWS, 1) for b in range(STEPS)], axis=0
            )
            put(lev, h, sb[lev, :CELLS, :] + end_scale * ends)

    @pl.when(jnp.logical_not(polar))
    def _():
        def put(lev, h, value):
            sb[lev, :CELLS, :] = value

        outs = []
        for c in range(CHUNKS):
            if c:
                inner(c)
            borders(c, put)
            if c == 0:
                spread_nest()
            pair = pl.ds(PAIR * c, PAIR)
            copy = pltpu.make_async_copy(sb.at[pair, pl.ds(0, SEG)], sect.at[pair], osem.at[c])
            copy.start()
            outs.append(copy)
        swap_nest()
        for copy in outs:
            copy.wait()
        for copy in tables:
            copy.wait()

    @pl.when(polar)
    def _():
        def put(c, lev, h, value):
            hi, lo = hi_lo(value)
            sh[c, :CELLS, h * ROWS : (h + 1) * ROWS] = hi
            sl[c, :CELLS, h * ROWS : (h + 1) * ROWS] = lo

        block = lanes((PART, ROWS)) // 32

        def exchange(c, k, src, dst, send, receive):
            return pltpu.make_async_remote_copy(
                src_ref=src.at[c, lax.rem(lon + k, SEGS)], dst_ref=dst.at[c, lon], send_sem=send.at[c, k],
                recv_sem=receive.at[c, k], device_id=(lat, lax.rem(lon + k, SEGS)), device_id_type=MESH,
            )

        there = []
        for c in range(CHUNKS):
            if c:
                inner(c)
            borders(c, functools.partial(put, c))
            if c == 0:
                tables[0].wait()
            both = dot(ut[...], sh[c])
            y = both[:RANK] + both[RANK:] + dot(ut[:RANK, :], sl[c])
            for h in range(PAIR):
                for q in range(4):
                    acc = None
                    for j in range(4):
                        v = y[PART * j : PART * (j + 1), ROWS * h : ROWS * (h + 1)]
                        if j != q:
                            v = pltpu.roll(v, (32 * (j - q)) % ROWS, 1)
                        acc = v if acc is None else jnp.where(block == j, v, acc)
                    fsend[c, 4 * h + q] = acc
            recv[c, lon] = fsend[c, lon]
            there.append([exchange(c, k, fsend, recv, fs, fr) for k in range(1, SEGS)])
            for copy in there[c]:
                copy.start()
            if c == 0:
                spread_nest()

        tables[1].wait()
        tables[2].wait()
        rows_cut = pltpu.roll(jnp.broadcast_to(cut[pl.ds(lat, 1), :], (8, ROWS)), ROWS - 32 * lax.rem(lon, 4), 1)[:1]
        n = lax.broadcasted_iota(jnp.int32, (256, ROWS), 0)
        root = math.sqrt(0.5)
        back, own = [], []
        for c in range(CHUNKS):
            for copy in there[c]:
                copy.wait_recv()
            y = [recv[c, d] for d in range(SEGS)]
            u = [y[j] + y[j + 4] for j in range(4)]
            v = [y[j] - y[j + 4] for j in range(4)]
            a, b, m, p = u[0] + u[2], u[1] + u[3], root * (v[1] - v[3]), root * (v[1] + v[3])
            groups = [(a + b, a - b), (v[0] + m, -v[2] - p), (u[0] - u[2], u[3] - u[1]), (v[0] - m, v[2] - p)]
            spectra = []
            for g, two in enumerate(groups):
                tall = jnp.concatenate(
                    [x if j == 0 else pltpu.roll(x, ROWS - 32 * j, 1) for x in two for j in range(4)], axis=0
                )
                wave = split_dot(pt[g], tall)
                number = 8 * (n & 63) + jnp.where((n & 64) == 0, g, 4 if g == 0 else 8 - g)
                wave = jnp.where(number <= rows_cut, wave, 0.0)
                full = split_dot(qt[g], wave)
                for x in range(2):
                    acc = None
                    for j in range(4):
                        w = full[RANK * x + PART * j : RANK * x + PART * (j + 1)]
                        if j:
                            w = pltpu.roll(w, 32 * j, 1)
                        acc = w if acc is None else jnp.where(block == j, w, acc)
                    spectra.append(acc)
            w0, w4, r1, i1, r2, i2, r3, i3 = spectra
            plus, minus = w0 + w4, w0 - w4
            evens = [plus + r2, minus - i2, plus - r2, minus + i2]
            d1, d2 = root * (r1 - r3), root * (i1 + i3)
            odds = [r1 + r3, d1 - d2, i3 - i1, -d1 - d2]
            for e in range(4):
                bsend[c, e] = evens[e] + odds[e]
                bsend[c, e + 4] = evens[e] - odds[e]
            back.append([exchange(c, k, bsend, zout, bs, br) for k in range(1, SEGS)])
            for copy in back[c]:
                copy.start()
            copy = pltpu.make_async_copy(bsend.at[c, lon], zout.at[c, lon], zsem.at[c])
            copy.start()
            own.append(copy)
        swap_nest()
        for c in range(CHUNKS):
            own[c].wait()
            for copy in back[c]:
                copy.wait_recv()
        for c in range(CHUNKS):
            for copy in there[c] + back[c]:
                copy.wait_send()

    swap.wait()
    for copy in lon_copies + nest_copies + spread:
        copy.wait_send()
    for n, copy in enumerate(lat_copies):
        pl.when((has_after, has_before)[n % 2])(copy.wait_send)


def finish_kernel(corners, zin, eu, sect, nestg, out, ob, nb, zc, osem, ssem, nsem):
    lat, lon = lax.axis_index("lat"), lax.axis_index("lon")
    polar = (lat < BANDS // 4) | (lat >= BANDS - BANDS // 4)
    half = lat // (BANDS // 2)
    row = corners[half, 0] - lat * ROWS
    col = corners[half, 1] - lon * SEG
    hit = (row > -ROWS) & (row < ROWS) & (col > -256) & (col < SEG)
    miss = jnp.logical_not(hit)
    fetch = pltpu.make_async_copy(nestg, nb, nsem)
    copies = [
        pltpu.make_async_copy(
            ob.at[pl.ds(PAIR * c, PAIR), pl.ds(256, SEG), :], out.at[pl.ds(PAIR * c, PAIR)], osem.at[c]
        )
        for c in range(CHUNKS)
    ]
    fills = [
        pltpu.make_async_copy(
            sect.at[pl.ds(PAIR * c, PAIR)], ob.at[pl.ds(PAIR * c, PAIR), pl.ds(256, SEG), :], ssem.at[c]
        )
        for c in range(CHUNKS)
    ]
    block = lanes((PART, ROWS)) // 32

    @pl.when(jnp.logical_not(polar))
    def _():
        for copy in fills:
            copy.start()

    @pl.when(hit)
    def _():
        fetch.start()

    @pl.when(jnp.logical_not(polar))
    def _():
        for c in range(CHUNKS):
            fills[c].wait()

            @pl.when(miss)
            def _():
                copies[c].start()

    @pl.when(polar)
    def _():
        for c in range(CHUNKS):
            for h in range(PAIR):
                for j in range(4):
                    acc = None
                    for q in range(4):
                        v = zin[c, 4 * h + q]
                        if j != q:
                            v = pltpu.roll(v, (32 * (q - j)) % ROWS, 1)
                        acc = v if acc is None else jnp.where(block == q, v, acc)
                    zc[PART * j : PART * (j + 1), h * ROWS : (h + 1) * ROWS] = acc
            hi, lo = hi_lo(zc[...])
            rhs = jnp.concatenate([hi, lo, hi, jnp.zeros((32, 2 * ROWS), jnp.bfloat16)], axis=0)
            full = dot(eu[...], rhs)
            for h in range(PAIR):
                ob[PAIR * c + h, 256 : 256 + CELLS, :] = full[:, h * ROWS : (h + 1) * ROWS]

            @pl.when(miss)
            def _():
                copies[c].start()

    @pl.when(hit)
    def _():
        fetch.wait()
        lane = lanes((264, ROWS))
        cell = lax.broadcasted_iota(jnp.int32, (264, ROWS), 0)
        place = col + 256
        base = pl.multiple_of((place // 8) * 8, 8)
        off = place - base
        inside = (lane >= row) & (lane < row + ROWS) & (cell >= off) & (cell < off + 256)
        for lev in range(LEV):
            flat = jnp.swapaxes(nb[lev], 0, 1)
            tall = jnp.concatenate([flat, jnp.zeros((8, ROWS), jnp.float32)], axis=0)
            tall = pltpu.roll(pltpu.roll(tall, off, 0), lax.rem(row + ROWS, ROWS), 1)
            here = ob[lev, pl.ds(base, 264), :]
            ob[lev, pl.ds(base, 264), :] = jnp.where(inside, tall, here)
            if lev % PAIR == PAIR - 1:
                copies[lev // PAIR].start()

    for copy in copies:
        copy.wait()


def shards(start, sec, zon, mer, cutoffs, nest_values, nest_corners, tables):
    ut, eu, pt, qt, rc = (jnp.asarray(x) for x in tables)
    flip = lambda x: jnp.swapaxes(x, 1, 2)
    anywhere = pl.BlockSpec(memory_space=pl.ANY)
    vmem = pl.BlockSpec(memory_space=pltpu.VMEM)
    smem = pl.BlockSpec(memory_space=pltpu.SMEM)
    f32, bf = jnp.float32, jnp.bfloat16
    dma = pltpu.SemaphoreType.DMA
    field = pltpu.VMEM((LEV, TALL, ROWS), f32)
    zout, sect, nestg = pl.pallas_call(
        section_kernel,
        out_shape=(
            jax.ShapeDtypeStruct((CHUNKS, SEGS, PART, ROWS), f32),
            jax.ShapeDtypeStruct((LEV, SEG, ROWS), f32),
            jax.ShapeDtypeStruct((LEV, 128, 256), f32),
        ),
        in_specs=[anywhere] * 7 + [vmem] * 3,
        out_specs=(anywhere,) * 3,
        scratch_shapes=[
            field, field, field, field,
            pltpu.VMEM((2 * RANK, WIDE), bf), pltpu.VMEM((4, 256, 4 * RANK), bf), pltpu.VMEM((4, 2 * RANK, 512), bf),
            pltpu.VMEM((CHUNKS, WIDE, 256), bf), pltpu.VMEM((CHUNKS, WIDE, 256), bf),
            pltpu.VMEM((CHUNKS, 2, STEP, ROWS), f32), pltpu.VMEM((CHUNKS, 2, 2, STEP, ROWS), f32),
            pltpu.VMEM((2, 2, LEV, 1, ROWS), f32),
            pltpu.VMEM((CHUNKS, SEGS, PART, ROWS), f32), pltpu.VMEM((CHUNKS, SEGS, PART, ROWS), f32),
            pltpu.VMEM((CHUNKS, SEGS, PART, ROWS), f32),
            pltpu.VMEM((16, 256), f32), pltpu.VMEM((SEGS, 16, 256), f32), pltpu.VMEM((2, LEV, SEGS, 256), f32),
            dma((CHUNKS, 4)), dma((3,)), dma((CHUNKS, 2)), dma((CHUNKS, 2)), dma((2, 2)), dma((2, 2)),
            dma((CHUNKS, SEGS)), dma((CHUNKS, SEGS)), dma((CHUNKS, SEGS)), dma((CHUNKS, SEGS)),
            dma((SEGS,)), dma((SEGS,)), dma((BANDS,)), dma((BANDS,)), dma((LEV + 1,)), dma((CHUNKS,)),
        ],
        compiler_params=pltpu.CompilerParams(
            collective_id=0, has_side_effects=True, vmem_limit_bytes=56 * 2**20
        ),
        cost_estimate=pl.CostEstimate(flops=10**9, bytes_accessed=16 * 10**6, transcendentals=0),
    )(
        flip(start), flip(sec), flip(zon), flip(mer), ut, pt, qt,
        cutoffs.reshape(BANDS, ROWS), rc, nest_values,
    )
    result = pl.pallas_call(
        finish_kernel,
        out_shape=jax.ShapeDtypeStruct((LEV, SEG, ROWS), f32),
        in_specs=[smem, vmem, vmem, anywhere, anywhere],
        out_specs=anywhere,
        scratch_shapes=[
            pltpu.VMEM((LEV, 256 + 928 + 256, ROWS), f32),
            pltpu.VMEM((LEV, 128, 256), f32),
            pltpu.VMEM((RANK, 2 * ROWS), f32),
            dma((CHUNKS,)),
            dma((CHUNKS,)),
            dma,
        ],
        compiler_params=pltpu.CompilerParams(vmem_limit_bytes=56 * 2**20),
        cost_estimate=pl.CostEstimate(flops=10**9, bytes_accessed=4 * 10**6, transcendentals=0),
    )(nest_corners, zout, eu, sect, nestg)
    return flip(result)


def solution(mesh):
    tables = make_tables()
    spec = P(None, "lat", "lon")
    return jax.shard_map(
        lambda *args: shards(*args, tables),
        mesh=mesh,
        in_specs=(spec, spec, spec, spec, P(), P(None, None, ("lat", "lon"), None), P()),
        out_specs=spec,
        check_vma=False,
    )
```

```python
import functools
import math

import jax
import jax.numpy as jnp
import ml_dtypes
import numpy as np
from jax import lax
from jax.experimental import pallas as pl
from jax.experimental.pallas import tpu as pltpu
from jax.sharding import PartitionSpec as P

LEV, NLAT, NLON, KMAX = 6, 2048, 7200, 512
BANDS, SEGS = 16, 8
ROWS, SEG = NLAT // BANDS, NLON // SEGS
RANK = 160
PART = RANK // 4
CHUNKS, PAIR = 3, 2
STEP, STEPS = 32, 29
CELLS = STEP * STEPS
TALL = CELLS + 8
WIDE = 1024
FAR_FIRST = (4, 5, 3, 2, 6, 1, 7)
MESH = pl.DeviceIdType.MESH
BF = ml_dtypes.bfloat16


def tri_solve(diag, off, shift, rhs):
    n, r = rhs.shape
    b = rhs.copy()
    d, u1, u2 = (np.zeros((n, r)) for _ in range(3))
    cd, cu, cb = diag[0] - shift, np.full(r, off[0]), b[0]
    for j in range(n - 1):
        nd, nu, sub = diag[j + 1] - shift, off[j + 1] if j + 2 < n else 0.0, off[j]
        swap = np.abs(sub) > np.abs(cd)
        p = np.where(swap, sub, np.where(cd == 0, 1e-30, cd))
        pu1, pu2, pb = np.where(swap, nd, cu), np.where(swap, nu, 0.0), np.where(swap, b[j + 1], cb)
        o, ou1 = np.where(swap, cd, sub), np.where(swap, cu, nd)
        ou2, ob = np.where(swap, 0.0, nu), np.where(swap, cb, b[j + 1])
        f = o / p
        d[j], u1[j], u2[j], b[j] = p, pu1, pu2, pb
        cd, cu, cb = ou1 - f * pu1, ou2 - f * pu2, ob - f * pb
    d[n - 1] = np.where(np.abs(cd) < 1e-20, 1e-20, cd)
    b[n - 1] = cb
    x = np.zeros((n, r))
    x[n - 1] = b[n - 1] / d[n - 1]
    x[n - 2] = (b[n - 2] - u1[n - 2] * x[n - 1]) / d[n - 2]
    for j in range(n - 3, -1, -1):
        x[j] = (b[j] - u1[j] * x[j + 1] - u2[j] * x[j + 2]) / d[j]
    return x


def slepian(length, width, rank):
    i = np.arange(length, dtype=np.float64)
    diag = ((length - 1 - 2 * i) / 2) ** 2 * np.cos(2 * np.pi * width)
    off = (i * (length - i) / 2)[1:]
    off2 = np.concatenate([[0.0], off**2])
    bound = np.abs(diag).max() + 2 * off.max()
    low, high, want = np.full(rank, -bound), np.full(rank, bound), np.arange(rank)
    for _ in range(70):
        mid = 0.5 * (low + high)
        above, q = np.zeros(rank, dtype=np.int64), np.ones(rank)
        for j in range(length):
            q = diag[j] - mid - off2[j] / q
            q = np.where(q == 0.0, 1e-300, q)
            above += q > 0
        up = above > want
        low, high = np.where(up, mid, low), np.where(up, high, mid)
    x = np.ones((length, rank)) + 0.3 * np.cos(i * i)[:, None]
    for _ in range(4):
        x = tri_solve(diag, off, 0.5 * (low + high), x)
        x = x / np.sqrt((x * x).sum(0))
    return x


def split(x):
    hi = x.astype(BF)
    return hi, (x - hi.astype(np.float64)).astype(BF)


def make_tables():
    basis = slepian(SEG, 512.0 / NLON, RANK)
    k, i = np.arange(KMAX), np.arange(SEG)
    waves = np.exp(-2j * np.pi * ((i[:, None] * k[None, :]) % NLON) / NLON)
    v = np.einsum("ir,ik->rk", basis, waves)
    weight = np.where(k == 0, 1.0, 2.0) / NLON
    uh, ul = split(basis)
    ut = np.zeros((2 * RANK, WIDE), BF)
    ut[:RANK, :SEG], ut[RANK:, :SEG] = uh.T, ul.T
    eu = np.zeros((CELLS, 512), BF)
    eu[:SEG, :RANK], eu[:SEG, RANK : 2 * RANK], eu[:SEG, 2 * RANK : 3 * RANK] = uh, uh, ul
    pt = np.zeros((4, 256, 4 * RANK), BF)
    qt = np.zeros((4, 2 * RANK, 512), BF)
    for g in range(4):
        s1, s2 = g, (4 if g == 0 else 8 - g)
        k1, k2 = np.arange(64) * 8 + s1, np.arange(64) * 8 + s2
        v1, v2 = v[:, k1], v[:, k2]
        w1, w2 = weight[k1], weight[k2]
        z = np.zeros((RANK, 64))
        if g == 0:
            p = np.block([[v1.real, z, v1.imag, z], [z, v2.real, z, v2.imag]])
            q = np.block([[v1.real * w1, z, v1.imag * w1, z], [z, v2.real * w2, z, v2.imag * w2]])
        else:
            p = np.block([[v1.real, v2.real, v1.imag, v2.imag], [-v1.imag, v2.imag, v1.real, -v2.real]])
            q = np.block(
                [
                    [v1.real * w1, v2.real * w2, v1.imag * w1, v2.imag * w2],
                    [-v1.imag * w1, v2.imag * w2, v1.real * w1, -v2.real * w2],
                ]
            )
        ph, pl_ = split(p.T)
        pt[g, :, : 2 * RANK], pt[g, :, 2 * RANK :] = ph, pl_
        qh, ql = split(q)
        qt[g, :, :256], qt[g, :, 256:] = qh, ql
    step = np.float32(math.pi / NLAT)
    half = np.float32(math.pi / 2)
    e = np.arange(NLAT + 1)
    edge = np.cos((e.astype(np.float32) * step - half).astype(np.float64)).astype(np.float32)
    edge[0] = edge[-1] = 0.0
    center = np.cos(((np.arange(NLAT).astype(np.float32) + np.float32(0.5)) * step - half).astype(np.float64))
    rc = np.zeros((BANDS, 8, ROWS), np.float32)
    for b in range(BANDS):
        r0 = b * ROWS
        rc[b, 0, : ROWS - 1] = 0.0625 * edge[r0 + 1 : r0 + ROWS]
        rc[b, 1] = (1.0 / center[r0 : r0 + ROWS]).astype(np.float32)
        rc[b, 4, 0], rc[b, 4, ROWS - 1] = rc[b, 1, 0], -rc[b, 1, ROWS - 1]
        rc[b, 2] = 0.0625 * edge[r0]
        rc[b, 3] = 0.0625 * edge[r0 + ROWS]
    return ut, eu, pt, qt, rc


def lanes(shape):
    return lax.broadcasted_iota(jnp.int32, shape, len(shape) - 1)


def hi_lo(x):
    hi = x.astype(jnp.bfloat16)
    return hi, (x - hi.astype(jnp.float32)).astype(jnp.bfloat16)


def dot(a, b):
    return jnp.dot(a, b, preferred_element_type=jnp.float32)


def split_dot(table, x):
    hi, lo = hi_lo(x)
    rhs = jnp.concatenate(
        [jnp.concatenate([hi, lo], axis=1), jnp.concatenate([hi, jnp.zeros_like(lo)], axis=1)], axis=0
    )
    both = dot(table, rhs)
    return both[:, : x.shape[1]] + both[:, x.shape[1] :]


def section_kernel(
    start, sec, zon, mer, ut_h, pt_h, qt_h, cut_h, rc_h, nest_h,
    zout, sect, nestg,
    cut, rc, nest, sb, tb, zb, mb, ut, pt, qt, sh, sl, pk, pkr, lh,
    fsend, recv, bsend, nsend, ngat, nasm,
    ld, tabs, psend, precv, lsend, lrecv, fs, fr, bs, br, n1s, n1r, n2s, n2r, osem, zsem,
):
    lat, lon = lax.axis_index("lat"), lax.axis_index("lon")
    polar = (lat < BANDS // 4) | (lat >= BANDS - BANDS // 4)
    core = lax.rem(lon, 2)

    barrier = pltpu.get_barrier_semaphore()
    for k in range(1, SEGS):
        pl.semaphore_signal(barrier, inc=1, device_id=(lat, lax.rem(lon + k, SEGS)), device_id_type=MESH)
    for k in range(1, BANDS):
        pl.semaphore_signal(barrier, inc=1, device_id=(lax.rem(lat + k, BANDS), lon), device_id_type=MESH)

    loads = [
        [
            pltpu.make_async_copy(
                src.at[pl.ds(PAIR * c, PAIR)], dst.at[pl.ds(PAIR * c, PAIR), pl.ds(0, SEG)], ld.at[c, a]
            )
            for a, (src, dst) in enumerate(((sec, tb), (mer, mb), (zon, zb), (start, sb)))
        ]
        for c in range(CHUNKS)
    ]
    tables = [
        pltpu.make_async_copy(src, dst, tabs.at[n]) for n, (src, dst) in enumerate(((ut_h, ut), (pt_h, pt), (qt_h, qt)))
    ]
    small = [
        pltpu.make_async_copy(src, dst, tabs.at[3 + n])
        for n, (src, dst) in enumerate(((nest_h, nest), (rc_h.at[lat], rc), (cut_h, cut)))
    ]
    for copy in small + loads[0] + tables[:1] + loads[1] + loads[2] + tables[1:]:
        copy.start()

    for buf in (tb, zb, mb, sb):
        for lev in range(LEV):
            buf[lev, SEG:TALL, :] = jnp.zeros((TALL - SEG, ROWS), jnp.float32)
    for c in range(CHUNKS):
        sh[c, CELLS:, :] = jnp.zeros((WIDE - CELLS, 256), jnp.bfloat16)
        sl[c, CELLS:, :] = jnp.zeros((WIDE - CELLS, 256), jnp.bfloat16)

    lane = lanes((STEP, ROWS))
    even = (lane & 1) == 0
    before, after = lax.rem(lat + BANDS - 1, BANDS), lax.rem(lat + 1, BANDS)
    left, right = lax.rem(lon + SEGS - 1, SEGS), lax.rem(lon + 1, SEGS)
    has_before, has_after = lat > 0, lat < BANDS - 1
    lat_copies, lon_copies, nest_copies = [], [], []
    def send_halo(c):
        loads[c][0].wait()
        loads[c][1].wait()

        def pack(b, acc, c=c):
            out = []
            for buf, x in zip((tb, mb), acc):
                for h in range(PAIR):
                    v = buf[PAIR * c + h, pl.ds(pl.multiple_of(b * STEP, STEP), STEP), :]
                    x = jnp.where((lane >> 1) == 2 * b + h, pltpu.roll(v, lax.rem(4 * b + 2 * h + 1, ROWS), 1), x)
                out.append(x)
            return tuple(out)

        none = jnp.zeros((STEP, ROWS), jnp.float32)
        packed = lax.fori_loop(0, STEPS, pack, (none, none), unroll=True)
        for a in range(2):
            pk[c, a] = packed[a]
        if c == 0:
            pl.semaphore_wait(barrier, SEGS - 1 + BANDS - 1)
        for way, (to, there_is) in enumerate(((after, has_after), (before, has_before))):
            copy = pltpu.make_async_remote_copy(
                src_ref=pk.at[c], dst_ref=pkr.at[c, way], send_sem=psend.at[c, way], recv_sem=precv.at[c, way],
                device_id=(to, lon), device_id_type=MESH,
            )
            pl.when(there_is)(copy.start)
            lat_copies.append(copy)
        if c == 0:
            for a, src in enumerate((sec, zon)):
                for way, (row, to) in enumerate(((0, left), (SEG - 1, right))):
                    copy = pltpu.make_async_remote_copy(
                        src_ref=src.at[:, pl.ds(row, 1), :], dst_ref=lh.at[a, way], send_sem=lsend.at[a, way],
                        recv_sem=lrecv.at[a, way], device_id=(lat, to), device_id_type=MESH,
                    )
                    copy.start()
                    lon_copies.append(copy)

    send_halo(0)
    for way, there_is in enumerate((has_before, has_after)):

        @pl.when(jnp.logical_not(there_is))
        def _(way=way):
            for c in range(CHUNKS):
                for a in range(2):
                    pkr[c, way, a] = jnp.zeros((STEP, ROWS), jnp.float32)

    small[0].wait()
    for n in range(12):
        nsend[n : n + 1, :] = nest[n // 6, n % 6]
    nsend[12:16, :] = jnp.zeros((4, 256), jnp.float32)
    for k in range(1, SEGS):
        copy = pltpu.make_async_remote_copy(
            src_ref=nsend, dst_ref=ngat.at[lon], send_sem=n1s.at[k], recv_sem=n1r.at[k],
            device_id=(lat, lax.rem(lon + k, SEGS)), device_id_type=MESH,
        )
        copy.start()
        nest_copies.append(copy)
    ngat[lon] = nsend[...]

    small[1].wait()
    small[2].wait()
    edge_row, inverse_cos = rc[0:1, :], rc[1:2, :]
    first_edge, last_edge, end_scale = rc[2:3, :], rc[3:4, :], rc[4:5, :]
    flux_scale = jnp.where(even[:1], last_edge, first_edge)

    def inner(c):
        for copy in loads[c][2:]:
            copy.wait()
        for lev in range(PAIR * c, PAIR * c + PAIR):
            t_all, z_all = tb[lev], zb[lev]
            t = t_all[:CELLS]
            east = 0.0625 * (z_all[:CELLS] + z_all[1 : CELLS + 1]) * (t + t_all[1 : CELLS + 1])
            zonal = east - jnp.concatenate([jnp.zeros((1, ROWS), jnp.float32), east[: CELLS - 1]], axis=0)
            m = mb[lev, :CELLS, :]
            south = edge_row * (t + pltpu.roll(t, ROWS - 1, 1)) * (m + pltpu.roll(m, ROWS - 1, 1))
            north = pltpu.roll(south, 1, 1)
            sb[lev, :CELLS, :] = 0.75 * sb[lev, :CELLS, :] + 0.25 * t - zonal - inverse_cos * (south - north)

    inner(0)
    for c in range(1, CHUNKS):
        send_halo(c)

    eight = pl.ds(pl.multiple_of(lat * SEGS, SEGS), SEGS)
    mine, other = pl.ds(LEV // 2 * core, LEV // 2), pl.ds(LEV // 2 * (1 - core), LEV // 2)
    spread = []
    for k in range(1, BANDS):
        to = lax.rem(lat + k, BANDS)
        copy = pltpu.make_async_remote_copy(
            src_ref=nasm.at[to // (BANDS // 2), mine], dst_ref=nestg.at[mine, eight, :], send_sem=n2s.at[k],
            recv_sem=n2r.at[k], device_id=(to, lon), device_id_type=MESH,
        )
        spread.append(copy)
    own_nest = pltpu.make_async_copy(nasm.at[lat // (BANDS // 2), mine], nestg.at[mine, eight, :], osem.at[LEV])
    swap = pltpu.make_async_remote_copy(
        src_ref=nestg.at[mine], dst_ref=nestg.at[mine], send_sem=n2s.at[0], recv_sem=n2r.at[0],
        device_id=(lat, lon + 1 - 2 * core), device_id_type=MESH,
    )

    def spread_nest():
        for copy in nest_copies:
            copy.wait_recv()
        for n in range(12):
            nasm[n // 6, n % 6] = jnp.concatenate([ngat[d, n : n + 1, :] for d in range(SEGS)], axis=0)
        for copy in spread:
            copy.start()
        own_nest.start()

    def swap_nest():
        for copy in spread:
            copy.wait_recv()
        own_nest.wait()
        swap.start()

    def borders(c, put):
        if c == 0:
            for copy in lon_copies:
                copy.wait_recv()
        for way, there_is in enumerate((has_before, has_after)):
            pl.when(there_is)(lat_copies[2 * c + way].wait_recv)
        sums = [
            pk[c, a] + jnp.where(even, pltpu.roll(pkr[c, 1, a], ROWS - 1, 1), pltpu.roll(pkr[c, 0, a], 1, 1))
            for a in range(2)
        ]
        packed = sums[0] * sums[1] * flux_scale
        for h in range(PAIR):
            lev = PAIR * c + h
            t0, z0 = tb[lev, 0:1, :], zb[lev, 0:1, :]
            t1, z1 = tb[lev, SEG - 1 : SEG, :], zb[lev, SEG - 1 : SEG, :]
            west = 0.0625 * (lh[1, 1, lev] + z0) * (lh[0, 1, lev] + t0)
            east = 0.0625 * (lh[1, 0, lev] + z1) * (lh[0, 0, lev] + t1)
            sb[lev, 0:1, :] = sb[lev, 0:1, :] + west
            sb[lev, SEG - 1 : SEG, :] = sb[lev, SEG - 1 : SEG, :] - (east - 0.0625 * z1 * t1)
            ends = jnp.concatenate(
                [pltpu.roll(packed, (2 * ROWS - 1 - 4 * b - 2 * h) % ROWS, 1) for b in range(STEPS)], axis=0
            )
            put(lev, h, sb[lev, :CELLS, :] + end_scale * ends)

    @pl.when(jnp.logical_not(polar))
    def _():
        def put(lev, h, value):
            sb[lev, :CELLS, :] = value

        outs = []
        for c in range(CHUNKS):
            if c:
                inner(c)
            borders(c, put)
            if c == 0:
                spread_nest()
            pair = pl.ds(PAIR * c, PAIR)
            copy = pltpu.make_async_copy(sb.at[pair, pl.ds(0, SEG)], sect.at[pair], osem.at[c])
            copy.start()
            outs.append(copy)
        swap_nest()
        for copy in outs:
            copy.wait()
        for copy in tables:
            copy.wait()

    @pl.when(polar)
    def _():
        def put(c, lev, h, value):
            hi, lo = hi_lo(value)
            sh[c, :CELLS, h * ROWS : (h + 1) * ROWS] = hi
            sl[c, :CELLS, h * ROWS : (h + 1) * ROWS] = lo

        block = lanes((PART, ROWS)) // 32

        def exchange(c, k, src, dst, send, receive):
            return pltpu.make_async_remote_copy(
                src_ref=src.at[c, lax.rem(lon + k, SEGS)], dst_ref=dst.at[c, lon], send_sem=send.at[c, k],
                recv_sem=receive.at[c, k], device_id=(lat, lax.rem(lon + k, SEGS)), device_id_type=MESH,
            )

        there = []
        for c in range(CHUNKS):
            if c:
                inner(c)
            borders(c, functools.partial(put, c))
            if c == 0:
                tables[0].wait()
            both = dot(ut[...], sh[c])
            y = both[:RANK] + both[RANK:] + dot(ut[:RANK, :], sl[c])
            for h in range(PAIR):
                for q in range(4):
                    acc = None
                    for j in range(4):
                        v = y[PART * j : PART * (j + 1), ROWS * h : ROWS * (h + 1)]
                        if j != q:
                            v = pltpu.roll(v, (32 * (j - q)) % ROWS, 1)
                        acc = v if acc is None else jnp.where(block == j, v, acc)
                    fsend[c, 4 * h + q] = acc
            recv[c, lon] = fsend[c, lon]
            there.append([exchange(c, k, fsend, recv, fs, fr) for k in FAR_FIRST])
            for copy in there[c]:
                copy.start()
            if c == 0:
                spread_nest()

        tables[1].wait()
        tables[2].wait()
        rows_cut = pltpu.roll(jnp.broadcast_to(cut[pl.ds(lat, 1), :], (8, ROWS)), ROWS - 32 * lax.rem(lon, 4), 1)[:1]
        n = lax.broadcasted_iota(jnp.int32, (256, ROWS), 0)
        root = math.sqrt(0.5)
        back, own = [], []
        for c in range(CHUNKS):
            for copy in there[c]:
                copy.wait_recv()
            y = [recv[c, d] for d in range(SEGS)]
            u = [y[j] + y[j + 4] for j in range(4)]
            v = [y[j] - y[j + 4] for j in range(4)]
            a, b, m, p = u[0] + u[2], u[1] + u[3], root * (v[1] - v[3]), root * (v[1] + v[3])
            groups = [(a + b, a - b), (v[0] + m, -v[2] - p), (u[0] - u[2], u[3] - u[1]), (v[0] - m, v[2] - p)]
            spectra = []
            for g, two in enumerate(groups):
                tall = jnp.concatenate(
                    [x if j == 0 else pltpu.roll(x, ROWS - 32 * j, 1) for x in two for j in range(4)], axis=0
                )
                wave = split_dot(pt[g], tall)
                number = 8 * (n & 63) + jnp.where((n & 64) == 0, g, 4 if g == 0 else 8 - g)
                wave = jnp.where(number <= rows_cut, wave, 0.0)
                full = split_dot(qt[g], wave)
                for x in range(2):
                    acc = None
                    for j in range(4):
                        w = full[RANK * x + PART * j : RANK * x + PART * (j + 1)]
                        if j:
                            w = pltpu.roll(w, 32 * j, 1)
                        acc = w if acc is None else jnp.where(block == j, w, acc)
                    spectra.append(acc)
            w0, w4, r1, i1, r2, i2, r3, i3 = spectra
            plus, minus = w0 + w4, w0 - w4
            evens = [plus + r2, minus - i2, plus - r2, minus + i2]
            d1, d2 = root * (r1 - r3), root * (i1 + i3)
            odds = [r1 + r3, d1 - d2, i3 - i1, -d1 - d2]
            for e in range(4):
                bsend[c, e] = evens[e] + odds[e]
                bsend[c, e + 4] = evens[e] - odds[e]
            back.append([exchange(c, k, bsend, zout, bs, br) for k in FAR_FIRST])
            for copy in back[c]:
                copy.start()
            copy = pltpu.make_async_copy(bsend.at[c, lon], zout.at[c, lon], zsem.at[c])
            copy.start()
            own.append(copy)
        swap_nest()
        for c in range(CHUNKS):
            own[c].wait()
            for copy in back[c]:
                copy.wait_recv()
        for c in range(CHUNKS):
            for copy in there[c] + back[c]:
                copy.wait_send()

    swap.wait()
    for copy in lon_copies + nest_copies + spread:
        copy.wait_send()
    for n, copy in enumerate(lat_copies):
        pl.when((has_after, has_before)[n % 2])(copy.wait_send)


def finish_kernel(corners, zin, eu, sect, nestg, out, ob, nb, zc, osem, ssem, nsem):
    lat, lon = lax.axis_index("lat"), lax.axis_index("lon")
    polar = (lat < BANDS // 4) | (lat >= BANDS - BANDS // 4)
    half = lat // (BANDS // 2)
    row = corners[half, 0] - lat * ROWS
    col = corners[half, 1] - lon * SEG
    hit = (row > -ROWS) & (row < ROWS) & (col > -256) & (col < SEG)
    miss = jnp.logical_not(hit)
    fetch = pltpu.make_async_copy(nestg, nb, nsem)
    copies = [
        pltpu.make_async_copy(
            ob.at[pl.ds(PAIR * c, PAIR), pl.ds(256, SEG), :], out.at[pl.ds(PAIR * c, PAIR)], osem.at[c]
        )
        for c in range(CHUNKS)
    ]
    fills = [
        pltpu.make_async_copy(
            sect.at[pl.ds(PAIR * c, PAIR)], ob.at[pl.ds(PAIR * c, PAIR), pl.ds(256, SEG), :], ssem.at[c]
        )
        for c in range(CHUNKS)
    ]
    block = lanes((PART, ROWS)) // 32

    @pl.when(jnp.logical_not(polar))
    def _():
        for copy in fills:
            copy.start()

    @pl.when(hit)
    def _():
        fetch.start()

    @pl.when(jnp.logical_not(polar))
    def _():
        for c in range(CHUNKS):
            fills[c].wait()

            @pl.when(miss)
            def _():
                copies[c].start()

    @pl.when(polar)
    def _():
        for c in range(CHUNKS):
            for h in range(PAIR):
                for j in range(4):
                    acc = None
                    for q in range(4):
                        v = zin[c, 4 * h + q]
                        if j != q:
                            v = pltpu.roll(v, (32 * (q - j)) % ROWS, 1)
                        acc = v if acc is None else jnp.where(block == q, v, acc)
                    zc[PART * j : PART * (j + 1), h * ROWS : (h + 1) * ROWS] = acc
            hi, lo = hi_lo(zc[...])
            rhs = jnp.concatenate([hi, lo, hi, jnp.zeros((32, 2 * ROWS), jnp.bfloat16)], axis=0)
            full = dot(eu[...], rhs)
            for h in range(PAIR):
                ob[PAIR * c + h, 256 : 256 + CELLS, :] = full[:, h * ROWS : (h + 1) * ROWS]

            @pl.when(miss)
            def _():
                copies[c].start()

    @pl.when(hit)
    def _():
        fetch.wait()
        lane = lanes((264, ROWS))
        cell = lax.broadcasted_iota(jnp.int32, (264, ROWS), 0)
        place = col + 256
        base = pl.multiple_of((place // 8) * 8, 8)
        off = place - base
        inside = (lane >= row) & (lane < row + ROWS) & (cell >= off) & (cell < off + 256)
        for lev in range(LEV):
            flat = jnp.swapaxes(nb[lev], 0, 1)
            tall = jnp.concatenate([flat, jnp.zeros((8, ROWS), jnp.float32)], axis=0)
            tall = pltpu.roll(pltpu.roll(tall, off, 0), lax.rem(row + ROWS, ROWS), 1)
            here = ob[lev, pl.ds(base, 264), :]
            ob[lev, pl.ds(base, 264), :] = jnp.where(inside, tall, here)
            if lev % PAIR == PAIR - 1:
                copies[lev // PAIR].start()

    for copy in copies:
        copy.wait()


def shards(start, sec, zon, mer, cutoffs, nest_values, nest_corners, tables):
    ut, eu, pt, qt, rc = (jnp.asarray(x) for x in tables)
    flip = lambda x: jnp.swapaxes(x, 1, 2)
    anywhere = pl.BlockSpec(memory_space=pl.ANY)
    vmem = pl.BlockSpec(memory_space=pltpu.VMEM)
    smem = pl.BlockSpec(memory_space=pltpu.SMEM)
    f32, bf = jnp.float32, jnp.bfloat16
    dma = pltpu.SemaphoreType.DMA
    field = pltpu.VMEM((LEV, TALL, ROWS), f32)
    zout, sect, nestg = pl.pallas_call(
        section_kernel,
        out_shape=(
            jax.ShapeDtypeStruct((CHUNKS, SEGS, PART, ROWS), f32),
            jax.ShapeDtypeStruct((LEV, SEG, ROWS), f32),
            jax.ShapeDtypeStruct((LEV, 128, 256), f32),
        ),
        in_specs=[anywhere] * 10,
        out_specs=(anywhere,) * 3,
        scratch_shapes=[
            pltpu.VMEM((BANDS, ROWS), jnp.int32), pltpu.VMEM((8, ROWS), f32), pltpu.VMEM((2, LEV, 1, 256), f32),
            field, field, field, field,
            pltpu.VMEM((2 * RANK, WIDE), bf), pltpu.VMEM((4, 256, 4 * RANK), bf), pltpu.VMEM((4, 2 * RANK, 512), bf),
            pltpu.VMEM((CHUNKS, WIDE, 256), bf), pltpu.VMEM((CHUNKS, WIDE, 256), bf),
            pltpu.VMEM((CHUNKS, 2, STEP, ROWS), f32), pltpu.VMEM((CHUNKS, 2, 2, STEP, ROWS), f32),
            pltpu.VMEM((2, 2, LEV, 1, ROWS), f32),
            pltpu.VMEM((CHUNKS, SEGS, PART, ROWS), f32), pltpu.VMEM((CHUNKS, SEGS, PART, ROWS), f32),
            pltpu.VMEM((CHUNKS, SEGS, PART, ROWS), f32),
            pltpu.VMEM((16, 256), f32), pltpu.VMEM((SEGS, 16, 256), f32), pltpu.VMEM((2, LEV, SEGS, 256), f32),
            dma((CHUNKS, 4)), dma((6,)), dma((CHUNKS, 2)), dma((CHUNKS, 2)), dma((2, 2)), dma((2, 2)),
            dma((CHUNKS, SEGS)), dma((CHUNKS, SEGS)), dma((CHUNKS, SEGS)), dma((CHUNKS, SEGS)),
            dma((SEGS,)), dma((SEGS,)), dma((BANDS,)), dma((BANDS,)), dma((LEV + 1,)), dma((CHUNKS,)),
        ],
        compiler_params=pltpu.CompilerParams(
            collective_id=0, has_side_effects=True, vmem_limit_bytes=56 * 2**20
        ),
        cost_estimate=pl.CostEstimate(flops=10**9, bytes_accessed=16 * 10**6, transcendentals=0),
    )(
        flip(start), flip(sec), flip(zon), flip(mer), ut, pt, qt,
        cutoffs.reshape(BANDS, ROWS), rc, nest_values,
    )
    result = pl.pallas_call(
        finish_kernel,
        out_shape=jax.ShapeDtypeStruct((LEV, SEG, ROWS), f32),
        in_specs=[smem, vmem, vmem, anywhere, anywhere],
        out_specs=anywhere,
        scratch_shapes=[
            pltpu.VMEM((LEV, 256 + 928 + 256, ROWS), f32),
            pltpu.VMEM((LEV, 128, 256), f32),
            pltpu.VMEM((RANK, 2 * ROWS), f32),
            dma((CHUNKS,)),
            dma((CHUNKS,)),
            dma,
        ],
        compiler_params=pltpu.CompilerParams(vmem_limit_bytes=56 * 2**20),
        cost_estimate=pl.CostEstimate(flops=10**9, bytes_accessed=4 * 10**6, transcendentals=0),
    )(nest_corners, zout, eu, sect, nestg)
    return flip(result)


def solution(mesh):
    tables = make_tables()
    spec = P(None, "lat", "lon")
    return jax.shard_map(
        lambda *args: shards(*args, tables),
        mesh=mesh,
        in_specs=(spec, spec, spec, spec, P(), P(None, None, ("lat", "lon"), None), P()),
        out_specs=spec,
        check_vma=False,
    )
```

```python
import functools
import math

import jax
import jax.numpy as jnp
import ml_dtypes
import numpy as np
from jax import lax
from jax.experimental import pallas as pl
from jax.experimental.pallas import tpu as pltpu
from jax.sharding import PartitionSpec as P

LEV, NLAT, NLON, KMAX = 6, 2048, 7200, 512
BANDS, SEGS = 16, 8
ROWS, SEG = NLAT // BANDS, NLON // SEGS
RANK = 160
PART = RANK // 4
CHUNKS, PAIR = 3, 2
STEP, STEPS = 32, 29
CELLS = STEP * STEPS
TALL = CELLS + 8
WIDE = 1024
FAR_FIRST = (4, 5, 3, 2, 6, 1, 7)
MESH = pl.DeviceIdType.MESH
BF = ml_dtypes.bfloat16


def tri_solve(diag, off, shift, rhs):
    n, r = rhs.shape
    b = rhs.copy()
    d, u1, u2 = (np.zeros((n, r)) for _ in range(3))
    cd, cu, cb = diag[0] - shift, np.full(r, off[0]), b[0]
    for j in range(n - 1):
        nd, nu, sub = diag[j + 1] - shift, off[j + 1] if j + 2 < n else 0.0, off[j]
        swap = np.abs(sub) > np.abs(cd)
        p = np.where(swap, sub, np.where(cd == 0, 1e-30, cd))
        pu1, pu2, pb = np.where(swap, nd, cu), np.where(swap, nu, 0.0), np.where(swap, b[j + 1], cb)
        o, ou1 = np.where(swap, cd, sub), np.where(swap, cu, nd)
        ou2, ob = np.where(swap, 0.0, nu), np.where(swap, cb, b[j + 1])
        f = o / p
        d[j], u1[j], u2[j], b[j] = p, pu1, pu2, pb
        cd, cu, cb = ou1 - f * pu1, ou2 - f * pu2, ob - f * pb
    d[n - 1] = np.where(np.abs(cd) < 1e-20, 1e-20, cd)
    b[n - 1] = cb
    x = np.zeros((n, r))
    x[n - 1] = b[n - 1] / d[n - 1]
    x[n - 2] = (b[n - 2] - u1[n - 2] * x[n - 1]) / d[n - 2]
    for j in range(n - 3, -1, -1):
        x[j] = (b[j] - u1[j] * x[j + 1] - u2[j] * x[j + 2]) / d[j]
    return x


def slepian(length, width, rank):
    i = np.arange(length, dtype=np.float64)
    diag = ((length - 1 - 2 * i) / 2) ** 2 * np.cos(2 * np.pi * width)
    off = (i * (length - i) / 2)[1:]
    off2 = np.concatenate([[0.0], off**2])
    bound = np.abs(diag).max() + 2 * off.max()
    low, high, want = np.full(rank, -bound), np.full(rank, bound), np.arange(rank)
    for _ in range(70):
        mid = 0.5 * (low + high)
        above, q = np.zeros(rank, dtype=np.int64), np.ones(rank)
        for j in range(length):
            q = diag[j] - mid - off2[j] / q
            q = np.where(q == 0.0, 1e-300, q)
            above += q > 0
        up = above > want
        low, high = np.where(up, mid, low), np.where(up, high, mid)
    x = np.ones((length, rank)) + 0.3 * np.cos(i * i)[:, None]
    for _ in range(4):
        x = tri_solve(diag, off, 0.5 * (low + high), x)
        x = x / np.sqrt((x * x).sum(0))
    return x


def split(x):
    hi = x.astype(BF)
    return hi, (x - hi.astype(np.float64)).astype(BF)


def make_tables():
    basis = slepian(SEG, 512.0 / NLON, RANK)
    k, i = np.arange(KMAX), np.arange(SEG)
    waves = np.exp(-2j * np.pi * ((i[:, None] * k[None, :]) % NLON) / NLON)
    v = np.einsum("ir,ik->rk", basis, waves)
    weight = np.where(k == 0, 1.0, 2.0) / NLON
    uh, ul = split(basis)
    ut = np.zeros((2 * RANK, WIDE), BF)
    ut[:RANK, :SEG], ut[RANK:, :SEG] = uh.T, ul.T
    eu = np.zeros((CELLS, 512), BF)
    eu[:SEG, :RANK], eu[:SEG, RANK : 2 * RANK], eu[:SEG, 2 * RANK : 3 * RANK] = uh, uh, ul
    pt = np.zeros((4, 256, 4 * RANK), BF)
    qt = np.zeros((4, 2 * RANK, 512), BF)
    for g in range(4):
        s1, s2 = g, (4 if g == 0 else 8 - g)
        k1, k2 = np.arange(64) * 8 + s1, np.arange(64) * 8 + s2
        v1, v2 = v[:, k1], v[:, k2]
        w1, w2 = weight[k1], weight[k2]
        z = np.zeros((RANK, 64))
        if g == 0:
            p = np.block([[v1.real, z, v1.imag, z], [z, v2.real, z, v2.imag]])
            q = np.block([[v1.real * w1, z, v1.imag * w1, z], [z, v2.real * w2, z, v2.imag * w2]])
        else:
            p = np.block([[v1.real, v2.real, v1.imag, v2.imag], [-v1.imag, v2.imag, v1.real, -v2.real]])
            q = np.block(
                [
                    [v1.real * w1, v2.real * w2, v1.imag * w1, v2.imag * w2],
                    [-v1.imag * w1, v2.imag * w2, v1.real * w1, -v2.real * w2],
                ]
            )
        ph, pl_ = split(p.T)
        pt[g, :, : 2 * RANK], pt[g, :, 2 * RANK :] = ph, pl_
        qh, ql = split(q)
        qt[g, :, :256], qt[g, :, 256:] = qh, ql
    step = np.float32(math.pi / NLAT)
    half = np.float32(math.pi / 2)
    e = np.arange(NLAT + 1)
    edge = np.cos((e.astype(np.float32) * step - half).astype(np.float64)).astype(np.float32)
    edge[0] = edge[-1] = 0.0
    center = np.cos(((np.arange(NLAT).astype(np.float32) + np.float32(0.5)) * step - half).astype(np.float64))
    rc = np.zeros((BANDS, 8, ROWS), np.float32)
    for b in range(BANDS):
        r0 = b * ROWS
        rc[b, 0, : ROWS - 1] = 0.0625 * edge[r0 + 1 : r0 + ROWS]
        rc[b, 1] = (1.0 / center[r0 : r0 + ROWS]).astype(np.float32)
        rc[b, 4, 0], rc[b, 4, ROWS - 1] = rc[b, 1, 0], -rc[b, 1, ROWS - 1]
        rc[b, 2] = 0.0625 * edge[r0]
        rc[b, 3] = 0.0625 * edge[r0 + ROWS]
    return ut, eu, pt, qt, rc


def lanes(shape):
    return lax.broadcasted_iota(jnp.int32, shape, len(shape) - 1)


def hi_lo(x):
    hi = x.astype(jnp.bfloat16)
    return hi, (x - hi.astype(jnp.float32)).astype(jnp.bfloat16)


def dot(a, b):
    return jnp.dot(a, b, preferred_element_type=jnp.float32)


def split_dot(table, x):
    hi, lo = hi_lo(x)
    rhs = jnp.concatenate(
        [jnp.concatenate([hi, lo], axis=1), jnp.concatenate([hi, jnp.zeros_like(lo)], axis=1)], axis=0
    )
    both = dot(table, rhs)
    return both[:, : x.shape[1]] + both[:, x.shape[1] :]


def section_kernel(
    start, sec, zon, mer, ut_h, pt_h, qt_h, cut_h, rc_h, nest_h,
    zout, sect, nestg,
    cut, rc, nest, sb, tb, zb, mb, ut, pt, qt, sh, sl, pk, pkr, lh,
    fsend, recv, bsend, nsend, ngat, nasm,
    ld, tabs, psend, precv, lsend, lrecv, fs, fr, bs, br, n1s, n1r, n2s, n2r, osem, zsem,
):
    lat, lon = lax.axis_index("lat"), lax.axis_index("lon")
    polar = (lat < BANDS // 4) | (lat >= BANDS - BANDS // 4)
    core = lax.rem(lon, 2)

    barrier = pltpu.get_barrier_semaphore()
    for k in range(1, SEGS):
        pl.semaphore_signal(barrier, inc=1, device_id=(lat, lax.rem(lon + k, SEGS)), device_id_type=MESH)
    for k in range(1, BANDS):
        pl.semaphore_signal(barrier, inc=1, device_id=(lax.rem(lat + k, BANDS), lon), device_id_type=MESH)

    loads = [
        [
            pltpu.make_async_copy(
                src.at[pl.ds(PAIR * c, PAIR)], dst.at[pl.ds(PAIR * c, PAIR), pl.ds(0, SEG)], ld.at[c, a]
            )
            for a, (src, dst) in enumerate(((sec, tb), (mer, mb), (zon, zb), (start, sb)))
        ]
        for c in range(CHUNKS)
    ]
    tables = [
        pltpu.make_async_copy(src, dst, tabs.at[n]) for n, (src, dst) in enumerate(((ut_h, ut), (pt_h, pt), (qt_h, qt)))
    ]
    small = [
        pltpu.make_async_copy(src, dst, tabs.at[3 + n])
        for n, (src, dst) in enumerate(((nest_h, nest), (rc_h.at[lat], rc), (cut_h, cut)))
    ]
    for copy in small + loads[0] + tables[:1] + loads[1] + loads[2] + tables[1:]:
        copy.start()

    for buf in (tb, zb, mb, sb):
        for lev in range(LEV):
            buf[lev, SEG:TALL, :] = jnp.zeros((TALL - SEG, ROWS), jnp.float32)
    for c in range(CHUNKS):
        sh[c, CELLS:, :] = jnp.zeros((WIDE - CELLS, 256), jnp.bfloat16)
        sl[c, CELLS:, :] = jnp.zeros((WIDE - CELLS, 256), jnp.bfloat16)

    lane = lanes((STEP, ROWS))
    even = (lane & 1) == 0
    before, after = lax.rem(lat + BANDS - 1, BANDS), lax.rem(lat + 1, BANDS)
    left, right = lax.rem(lon + SEGS - 1, SEGS), lax.rem(lon + 1, SEGS)
    has_before, has_after = lat > 0, lat < BANDS - 1
    lat_copies, lon_copies, nest_copies = [], [], []
    def send_halo(c):
        loads[c][0].wait()
        loads[c][1].wait()

        def pack(b, acc, c=c):
            out = []
            for buf, x in zip((tb, mb), acc):
                for h in range(PAIR):
                    v = buf[PAIR * c + h, pl.ds(pl.multiple_of(b * STEP, STEP), STEP), :]
                    x = jnp.where((lane >> 1) == 2 * b + h, pltpu.roll(v, lax.rem(4 * b + 2 * h + 1, ROWS), 1), x)
                out.append(x)
            return tuple(out)

        none = jnp.zeros((STEP, ROWS), jnp.float32)
        packed = lax.fori_loop(0, STEPS, pack, (none, none), unroll=True)
        for a in range(2):
            pk[c, a] = packed[a]
        if c == 0:
            pl.semaphore_wait(barrier, SEGS - 1 + BANDS - 1)
        for way, (to, there_is) in enumerate(((after, has_after), (before, has_before))):
            copy = pltpu.make_async_remote_copy(
                src_ref=pk.at[c], dst_ref=pkr.at[c, way], send_sem=psend.at[c, way], recv_sem=precv.at[c, way],
                device_id=(to, lon), device_id_type=MESH,
            )
            pl.when(there_is)(copy.start)
            lat_copies.append(copy)
        if c == 0:
            for a, src in enumerate((sec, zon)):
                for way, (row, to) in enumerate(((0, left), (SEG - 1, right))):
                    copy = pltpu.make_async_remote_copy(
                        src_ref=src.at[:, pl.ds(row, 1), :], dst_ref=lh.at[a, way], send_sem=lsend.at[a, way],
                        recv_sem=lrecv.at[a, way], device_id=(lat, to), device_id_type=MESH,
                    )
                    copy.start()
                    lon_copies.append(copy)

    send_halo(0)
    for way, there_is in enumerate((has_before, has_after)):

        @pl.when(jnp.logical_not(there_is))
        def _(way=way):
            for c in range(CHUNKS):
                for a in range(2):
                    pkr[c, way, a] = jnp.zeros((STEP, ROWS), jnp.float32)

    small[0].wait()
    for n in range(12):
        nsend[n : n + 1, :] = nest[n // 6, n % 6]
    nsend[12:16, :] = jnp.zeros((4, 256), jnp.float32)
    for k in range(1, SEGS):
        copy = pltpu.make_async_remote_copy(
            src_ref=nsend, dst_ref=ngat.at[lon], send_sem=n1s.at[k], recv_sem=n1r.at[k],
            device_id=(lat, lax.rem(lon + k, SEGS)), device_id_type=MESH,
        )
        copy.start()
        nest_copies.append(copy)
    ngat[lon] = nsend[...]

    small[1].wait()
    small[2].wait()
    edge_row, inverse_cos = rc[0:1, :], rc[1:2, :]
    first_edge, last_edge, end_scale = rc[2:3, :], rc[3:4, :], rc[4:5, :]
    flux_scale = jnp.where(even[:1], last_edge, first_edge)

    def inner(c):
        for copy in loads[c][2:]:
            copy.wait()
        for lev in range(PAIR * c, PAIR * c + PAIR):
            t_all, z_all = tb[lev], zb[lev]
            t = t_all[:CELLS]
            east = 0.0625 * (z_all[:CELLS] + z_all[1 : CELLS + 1]) * (t + t_all[1 : CELLS + 1])
            zonal = east - jnp.concatenate([jnp.zeros((1, ROWS), jnp.float32), east[: CELLS - 1]], axis=0)
            m = mb[lev, :CELLS, :]
            south = edge_row * (t + pltpu.roll(t, ROWS - 1, 1)) * (m + pltpu.roll(m, ROWS - 1, 1))
            north = pltpu.roll(south, 1, 1)
            sb[lev, :CELLS, :] = 0.75 * sb[lev, :CELLS, :] + 0.25 * t - zonal - inverse_cos * (south - north)

    inner(0)
    for c in range(1, CHUNKS):
        send_halo(c)

    eight = pl.ds(pl.multiple_of(lat * SEGS, SEGS), SEGS)
    mine, other = pl.ds(LEV // 2 * core, LEV // 2), pl.ds(LEV // 2 * (1 - core), LEV // 2)
    spread = []
    for k in range(1, BANDS):
        to = lax.rem(lat + k, BANDS)
        copy = pltpu.make_async_remote_copy(
            src_ref=nasm.at[to // (BANDS // 2), mine], dst_ref=nestg.at[mine, eight, :], send_sem=n2s.at[k],
            recv_sem=n2r.at[k], device_id=(to, lon), device_id_type=MESH,
        )
        spread.append(copy)
    own_nest = pltpu.make_async_copy(nasm.at[lat // (BANDS // 2), mine], nestg.at[mine, eight, :], osem.at[LEV])
    swap = pltpu.make_async_remote_copy(
        src_ref=nestg.at[mine], dst_ref=nestg.at[mine], send_sem=n2s.at[0], recv_sem=n2r.at[0],
        device_id=(lat, lon + 1 - 2 * core), device_id_type=MESH,
    )

    def spread_nest():
        for copy in nest_copies:
            copy.wait_recv()
        for n in range(12):
            nasm[n // 6, n % 6] = jnp.concatenate([ngat[d, n : n + 1, :] for d in range(SEGS)], axis=0)
        for copy in spread:
            copy.start()
        own_nest.start()

    def swap_nest():
        for copy in spread:
            copy.wait_recv()
        own_nest.wait()
        swap.start()

    def borders(c, put):
        if c == 0:
            for copy in lon_copies:
                copy.wait_recv()
        for way, there_is in enumerate((has_before, has_after)):
            pl.when(there_is)(lat_copies[2 * c + way].wait_recv)
        sums = [
            pk[c, a] + jnp.where(even, pltpu.roll(pkr[c, 1, a], ROWS - 1, 1), pltpu.roll(pkr[c, 0, a], 1, 1))
            for a in range(2)
        ]
        packed = sums[0] * sums[1] * flux_scale
        for h in range(PAIR):
            lev = PAIR * c + h
            t0, z0 = tb[lev, 0:1, :], zb[lev, 0:1, :]
            t1, z1 = tb[lev, SEG - 1 : SEG, :], zb[lev, SEG - 1 : SEG, :]
            west = 0.0625 * (lh[1, 1, lev] + z0) * (lh[0, 1, lev] + t0)
            east = 0.0625 * (lh[1, 0, lev] + z1) * (lh[0, 0, lev] + t1)
            sb[lev, 0:1, :] = sb[lev, 0:1, :] + west
            sb[lev, SEG - 1 : SEG, :] = sb[lev, SEG - 1 : SEG, :] - (east - 0.0625 * z1 * t1)
            ends = jnp.concatenate(
                [pltpu.roll(packed, (2 * ROWS - 1 - 4 * b - 2 * h) % ROWS, 1) for b in range(STEPS)], axis=0
            )
            put(lev, h, sb[lev, :CELLS, :] + end_scale * ends)

    @pl.when(jnp.logical_not(polar))
    def _():
        def put(lev, h, value):
            sb[lev, :CELLS, :] = value

        outs = []
        for c in range(CHUNKS):
            if c:
                inner(c)
            borders(c, put)
            if c == 0:
                spread_nest()
            pair = pl.ds(PAIR * c, PAIR)
            copy = pltpu.make_async_copy(sb.at[pair, pl.ds(0, SEG)], sect.at[pair], osem.at[c])
            copy.start()
            outs.append(copy)
        swap_nest()
        for copy in outs:
            copy.wait()
        for copy in tables:
            copy.wait()

    @pl.when(polar)
    def _():
        def put(c, lev, h, value):
            hi, lo = hi_lo(value)
            sh[c, :CELLS, h * ROWS : (h + 1) * ROWS] = hi
            sl[c, :CELLS, h * ROWS : (h + 1) * ROWS] = lo

        block = lanes((PART, ROWS)) // 32

        def exchange(c, k, src, dst, send, receive):
            return pltpu.make_async_remote_copy(
                src_ref=src.at[c, lax.rem(lon + k, SEGS)], dst_ref=dst.at[c, lon], send_sem=send.at[c, k],
                recv_sem=receive.at[c, k], device_id=(lat, lax.rem(lon + k, SEGS)), device_id_type=MESH,
            )

        there = []
        for c in range(CHUNKS):
            if c:
                inner(c)
            borders(c, functools.partial(put, c))
            if c == 0:
                tables[0].wait()
            both = dot(ut[...], sh[c])
            y = both[:RANK] + both[RANK:] + dot(ut[:RANK, :], sl[c])
            there.append([exchange(c, k, fsend, recv, fs, fr) for k in FAR_FIRST])
            for h in range(PAIR):
                for q in range(4):
                    acc = None
                    for j in range(4):
                        v = y[PART * j : PART * (j + 1), ROWS * h : ROWS * (h + 1)]
                        if j != q:
                            v = pltpu.roll(v, (32 * (j - q)) % ROWS, 1)
                        acc = v if acc is None else jnp.where(block == j, v, acc)
                    fsend[c, 4 * h + q] = acc
                for k, copy in zip(FAR_FIRST, there[c]):
                    pl.when(lax.rem(lon + k, SEGS) // 4 == h)(copy.start)
            recv[c, lon] = fsend[c, lon]
            if c == 0:
                spread_nest()

        tables[1].wait()
        tables[2].wait()
        rows_cut = pltpu.roll(jnp.broadcast_to(cut[pl.ds(lat, 1), :], (8, ROWS)), ROWS - 32 * lax.rem(lon, 4), 1)[:1]
        n = lax.broadcasted_iota(jnp.int32, (256, ROWS), 0)
        root = math.sqrt(0.5)
        back, own = [], []
        for c in range(CHUNKS):
            for copy in there[c]:
                copy.wait_recv()
            y = [recv[c, d] for d in range(SEGS)]
            u = [y[j] + y[j + 4] for j in range(4)]
            v = [y[j] - y[j + 4] for j in range(4)]
            a, b, m, p = u[0] + u[2], u[1] + u[3], root * (v[1] - v[3]), root * (v[1] + v[3])
            groups = [(a + b, a - b), (v[0] + m, -v[2] - p), (u[0] - u[2], u[3] - u[1]), (v[0] - m, v[2] - p)]
            spectra = []
            for g, two in enumerate(groups):
                tall = jnp.concatenate(
                    [x if j == 0 else pltpu.roll(x, ROWS - 32 * j, 1) for x in two for j in range(4)], axis=0
                )
                wave = split_dot(pt[g], tall)
                number = 8 * (n & 63) + jnp.where((n & 64) == 0, g, 4 if g == 0 else 8 - g)
                wave = jnp.where(number <= rows_cut, wave, 0.0)
                full = split_dot(qt[g], wave)
                for x in range(2):
                    acc = None
                    for j in range(4):
                        w = full[RANK * x + PART * j : RANK * x + PART * (j + 1)]
                        if j:
                            w = pltpu.roll(w, 32 * j, 1)
                        acc = w if acc is None else jnp.where(block == j, w, acc)
                    spectra.append(acc)
            w0, w4, r1, i1, r2, i2, r3, i3 = spectra
            plus, minus = w0 + w4, w0 - w4
            evens = [plus + r2, minus - i2, plus - r2, minus + i2]
            d1, d2 = root * (r1 - r3), root * (i1 + i3)
            odds = [r1 + r3, d1 - d2, i3 - i1, -d1 - d2]
            for e in range(4):
                bsend[c, e] = evens[e] + odds[e]
                bsend[c, e + 4] = evens[e] - odds[e]
            back.append([exchange(c, k, bsend, zout, bs, br) for k in FAR_FIRST])
            for copy in back[c]:
                copy.start()
            copy = pltpu.make_async_copy(bsend.at[c, lon], zout.at[c, lon], zsem.at[c])
            copy.start()
            own.append(copy)
        swap_nest()
        for c in range(CHUNKS):
            own[c].wait()
            for copy in back[c]:
                copy.wait_recv()
        for c in range(CHUNKS):
            for copy in there[c] + back[c]:
                copy.wait_send()

    swap.wait()
    for copy in lon_copies + nest_copies + spread:
        copy.wait_send()
    for n, copy in enumerate(lat_copies):
        pl.when((has_after, has_before)[n % 2])(copy.wait_send)


def finish_kernel(corners, zin, eu, sect, nestg, out, ob, nb, zc, osem, ssem, nsem):
    lat, lon = lax.axis_index("lat"), lax.axis_index("lon")
    polar = (lat < BANDS // 4) | (lat >= BANDS - BANDS // 4)
    half = lat // (BANDS // 2)
    row = corners[half, 0] - lat * ROWS
    col = corners[half, 1] - lon * SEG
    hit = (row > -ROWS) & (row < ROWS) & (col > -256) & (col < SEG)
    miss = jnp.logical_not(hit)
    fetch = pltpu.make_async_copy(nestg, nb, nsem)
    copies = [
        pltpu.make_async_copy(
            ob.at[pl.ds(PAIR * c, PAIR), pl.ds(256, SEG), :], out.at[pl.ds(PAIR * c, PAIR)], osem.at[c]
        )
        for c in range(CHUNKS)
    ]
    fills = [
        pltpu.make_async_copy(
            sect.at[pl.ds(PAIR * c, PAIR)], ob.at[pl.ds(PAIR * c, PAIR), pl.ds(256, SEG), :], ssem.at[c]
        )
        for c in range(CHUNKS)
    ]
    block = lanes((PART, ROWS)) // 32

    @pl.when(jnp.logical_not(polar))
    def _():
        for copy in fills:
            copy.start()

    @pl.when(hit)
    def _():
        fetch.start()

    @pl.when(jnp.logical_not(polar))
    def _():
        for c in range(CHUNKS):
            fills[c].wait()

            @pl.when(miss)
            def _():
                copies[c].start()

    @pl.when(polar)
    def _():
        for c in range(CHUNKS):
            for h in range(PAIR):
                for j in range(4):
                    acc = None
                    for q in range(4):
                        v = zin[c, 4 * h + q]
                        if j != q:
                            v = pltpu.roll(v, (32 * (q - j)) % ROWS, 1)
                        acc = v if acc is None else jnp.where(block == q, v, acc)
                    zc[PART * j : PART * (j + 1), h * ROWS : (h + 1) * ROWS] = acc
            hi, lo = hi_lo(zc[...])
            rhs = jnp.concatenate([hi, lo, hi, jnp.zeros((32, 2 * ROWS), jnp.bfloat16)], axis=0)
            full = dot(eu[...], rhs)
            for h in range(PAIR):
                ob[PAIR * c + h, 256 : 256 + CELLS, :] = full[:, h * ROWS : (h + 1) * ROWS]

            @pl.when(miss)
            def _():
                copies[c].start()

    @pl.when(hit)
    def _():
        fetch.wait()
        lane = lanes((264, ROWS))
        cell = lax.broadcasted_iota(jnp.int32, (264, ROWS), 0)
        place = col + 256
        base = pl.multiple_of((place // 8) * 8, 8)
        off = place - base
        inside = (lane >= row) & (lane < row + ROWS) & (cell >= off) & (cell < off + 256)
        for lev in range(LEV):
            flat = jnp.swapaxes(nb[lev], 0, 1)
            tall = jnp.concatenate([flat, jnp.zeros((8, ROWS), jnp.float32)], axis=0)
            tall = pltpu.roll(pltpu.roll(tall, off, 0), lax.rem(row + ROWS, ROWS), 1)
            here = ob[lev, pl.ds(base, 264), :]
            ob[lev, pl.ds(base, 264), :] = jnp.where(inside, tall, here)
            if lev % PAIR == PAIR - 1:
                copies[lev // PAIR].start()

    for copy in copies:
        copy.wait()


def shards(start, sec, zon, mer, cutoffs, nest_values, nest_corners, tables):
    ut, eu, pt, qt, rc = (jnp.asarray(x) for x in tables)
    flip = lambda x: jnp.swapaxes(x, 1, 2)
    anywhere = pl.BlockSpec(memory_space=pl.ANY)
    vmem = pl.BlockSpec(memory_space=pltpu.VMEM)
    smem = pl.BlockSpec(memory_space=pltpu.SMEM)
    f32, bf = jnp.float32, jnp.bfloat16
    dma = pltpu.SemaphoreType.DMA
    field = pltpu.VMEM((LEV, TALL, ROWS), f32)
    zout, sect, nestg = pl.pallas_call(
        section_kernel,
        out_shape=(
            jax.ShapeDtypeStruct((CHUNKS, SEGS, PART, ROWS), f32),
            jax.ShapeDtypeStruct((LEV, SEG, ROWS), f32),
            jax.ShapeDtypeStruct((LEV, 128, 256), f32),
        ),
        in_specs=[anywhere] * 10,
        out_specs=(anywhere,) * 3,
        scratch_shapes=[
            pltpu.VMEM((BANDS, ROWS), jnp.int32), pltpu.VMEM((8, ROWS), f32), pltpu.VMEM((2, LEV, 1, 256), f32),
            field, field, field, field,
            pltpu.VMEM((2 * RANK, WIDE), bf), pltpu.VMEM((4, 256, 4 * RANK), bf), pltpu.VMEM((4, 2 * RANK, 512), bf),
            pltpu.VMEM((CHUNKS, WIDE, 256), bf), pltpu.VMEM((CHUNKS, WIDE, 256), bf),
            pltpu.VMEM((CHUNKS, 2, STEP, ROWS), f32), pltpu.VMEM((CHUNKS, 2, 2, STEP, ROWS), f32),
            pltpu.VMEM((2, 2, LEV, 1, ROWS), f32),
            pltpu.VMEM((CHUNKS, SEGS, PART, ROWS), f32), pltpu.VMEM((CHUNKS, SEGS, PART, ROWS), f32),
            pltpu.VMEM((CHUNKS, SEGS, PART, ROWS), f32),
            pltpu.VMEM((16, 256), f32), pltpu.VMEM((SEGS, 16, 256), f32), pltpu.VMEM((2, LEV, SEGS, 256), f32),
            dma((CHUNKS, 4)), dma((6,)), dma((CHUNKS, 2)), dma((CHUNKS, 2)), dma((2, 2)), dma((2, 2)),
            dma((CHUNKS, SEGS)), dma((CHUNKS, SEGS)), dma((CHUNKS, SEGS)), dma((CHUNKS, SEGS)),
            dma((SEGS,)), dma((SEGS,)), dma((BANDS,)), dma((BANDS,)), dma((LEV + 1,)), dma((CHUNKS,)),
        ],
        compiler_params=pltpu.CompilerParams(
            collective_id=0, has_side_effects=True, vmem_limit_bytes=56 * 2**20
        ),
        cost_estimate=pl.CostEstimate(flops=10**9, bytes_accessed=16 * 10**6, transcendentals=0),
    )(
        flip(start), flip(sec), flip(zon), flip(mer), ut, pt, qt,
        cutoffs.reshape(BANDS, ROWS), rc, nest_values,
    )
    result = pl.pallas_call(
        finish_kernel,
        out_shape=jax.ShapeDtypeStruct((LEV, SEG, ROWS), f32),
        in_specs=[smem, vmem, vmem, anywhere, anywhere],
        out_specs=anywhere,
        scratch_shapes=[
            pltpu.VMEM((LEV, 256 + 928 + 256, ROWS), f32),
            pltpu.VMEM((LEV, 128, 256), f32),
            pltpu.VMEM((RANK, 2 * ROWS), f32),
            dma((CHUNKS,)),
            dma((CHUNKS,)),
            dma,
        ],
        compiler_params=pltpu.CompilerParams(vmem_limit_bytes=56 * 2**20),
        cost_estimate=pl.CostEstimate(flops=10**9, bytes_accessed=4 * 10**6, transcendentals=0),
    )(nest_corners, zout, eu, sect, nestg)
    return flip(result)


def solution(mesh):
    tables = make_tables()
    spec = P(None, "lat", "lon")
    return jax.shard_map(
        lambda *args: shards(*args, tables),
        mesh=mesh,
        in_specs=(spec, spec, spec, spec, P(), P(None, None, ("lat", "lon"), None), P()),
        out_specs=spec,
        check_vma=False,
    )
```
